32 devices in a mesh: groups: 2 (over y), slab: 4 (over z), dp: 4 (over x, core).
Axes of the slice: x: 2, y: 2, z: 4, core: 2. Of those that a mesh axis runs over, the one named last changes fastest.
Arguments:
- lattice_field: bfloat16 [8, 64, 8, 1024], P(('groups', 'dp'), None, 'slab'), parts along dimension 0, may hold values from -6 to 6
- fine_kernels: bfloat16 [2, 32, 32, 3, 3], P(None, 'dp'), may hold values from -0.375 to 0.375
- coarse_kernels: bfloat16 [2, 8, 8, 3, 3], P(None, 'dp'), may hold values from -0.75 to 0.75
Outputs:
- fine_latent: float32 [8, 64, 8, 1024], P(('groups', 'dp'), None, 'slab'), parts along dimension 0
- coarse_latent: float32 [8, 16, 4, 512], P(('groups', 'dp'), None, 'slab'), parts along dimension 0
- neg_log_density: float32 [8], P(('groups', 'dp')), parts along dimension 0
- fine_grads: float32 [4, 32, 32, 3, 3], P('groups', 'dp'), parts along dimension 0
- coarse_grads: float32 [4, 8, 8, 3, 3], P('groups', 'dp'), parts along dimension 0
The draws below stay inside these ranges and needn't reach their ends.
There are 2 independent parts, one for each index of `groups`. The reference program is written for one: setup_inputs(seed, part) draws one part's arguments, and reference() takes and returns one part's arrays. A program takes and returns all parts, laid end to end along the dimension named above; an argument that names none is the same for every part. Nothing has to cross between parts.
All inputs are finite; a program needn't handle non-finite values.
Results may differ from the reference program's by a relative error of at most 0.0025.
Values may be sent and summed in bfloat16 or wider, within the bound.
A program may use at most 128 MiB of HBM per device.

```python
import jax
import jax.numpy as jnp
from jax import lax

CH = 64
CC = 16
NF = 2
NC = 2
COLS = 1024
CH2 = 32
CC2 = 8
LATTICES = 4
HEIGHT = 8


def block_scale(rng, extent, pieces, smallest, largest):
    loudness = 1.0
    for dim, blocks in pieces:
        draws = jax.random.uniform(jax.random.fold_in(jax.random.fold_in(rng, 6), dim), (blocks,), jnp.float32, smallest / len(pieces), largest / len(pieces))
        loudness = loudness * jnp.repeat(jnp.exp(draws), extent[dim] // blocks).reshape((-1,) + (1,) * (len(extent) - 1 - dim))
    return loudness


def noise(rng, extent, scale, bound, cuts=(), dtype=jnp.bfloat16):
    loudness = block_scale(rng, extent, cuts, -0.22, 0.18) if cuts else 1.0
    entries = jax.random.normal(rng, extent, jnp.float32) * scale * loudness
    return jnp.minimum(jnp.maximum(entries, -bound), bound).astype(dtype)


def setup_inputs(seed: int = 0, part: int = 0) -> dict:
    splits = jax.random.split(jax.random.key(seed), 4)
    part_keys = jax.random.split(jax.random.fold_in(splits[3], part), 4)
    return {
        "lattice_field": noise(part_keys[0], (LATTICES, CH, HEIGHT, COLS), 1.0, 6.0, ((0, 4), (2, 4))),
        "fine_kernels": noise(splits[1], (NF, CH2, CH2, 3, 3), (9 * CH2) ** -0.5, 0.375, ((1, 4),)),
        "coarse_kernels": noise(splits[2], (NC, CC2, CC2, 3, 3), (9 * CC2) ** -0.5, 0.75, ((1, 4),)),
    }


FORWARD_NUMBERS = ("NCHW", "OIHW", "NCHW")


def correlate(padded, kernel):
    return lax.conv_general_dilated(padded, kernel, (1, 1), "VALID", dimension_numbers=FORWARD_NUMBERS, preferred_element_type=jnp.float32)


def spread_back(slope, kernel):
    widened = jnp.pad(slope, ((0, 0), (0, 0), (2, 2), (2, 2)))
    flipped = jnp.transpose(kernel[:, :, ::-1, ::-1], (1, 0, 2, 3))
    return correlate(widened, flipped)


def kernel_term(padded, slope):
    row_count, col_count = slope.shape[2], slope.shape[3]
    widened = padded.astype(jnp.float32)
    narrowed = slope.astype(jnp.float32)
    stacked_rows = []
    for offset_row in range(3):
        row_terms = [jnp.einsum("bcij,boij->oc", widened[:, :, offset_row:offset_row + row_count, offset_col:offset_col + col_count], narrowed) for offset_col in range(3)]
        stacked_rows.append(jnp.stack(row_terms, axis=-1))
    return jnp.stack(stacked_rows, axis=-2)


def wrap_both(condition):
    return jnp.pad(condition, ((0, 0), (0, 0), (1, 1), (1, 1)), mode="wrap")


def fold_wrap(gradient):
    interior = gradient[:, :, :, 1:-1]
    interior = interior.at[:, :, :, 0].add(gradient[:, :, :, -1]).at[:, :, :, -1].add(gradient[:, :, :, 0])
    trimmed = interior[:, :, 1:-1]
    return trimmed.at[:, :, 0].add(interior[:, :, -1]).at[:, :, -1].add(interior[:, :, 0])


def couple(current, kernel, layer_index, widener):
    half_count = current.shape[1] // 2
    if layer_index % 2 == 0:
        condition, moving = current[:, :half_count], current[:, half_count:]
    else:
        condition, moving = current[:, half_count:], current[:, :half_count]
    padded = widener(condition.astype(jnp.bfloat16))
    bent_part = jnp.tanh(correlate(padded, kernel))
    moving = moving + bent_part
    if layer_index % 2 == 0:
        joined = jnp.concatenate([condition, moving], axis=1)
    else:
        joined = jnp.concatenate([moving, condition], axis=1)
    return joined, (padded, bent_part)


def uncouple(gradient, kernel, layer_index, stored, narrower):
    padded, bent_part = stored
    half_count = gradient.shape[1] // 2
    if layer_index % 2 == 0:
        grad_cond, grad_moving = gradient[:, :half_count], gradient[:, half_count:]
    else:
        grad_cond, grad_moving = gradient[:, half_count:], gradient[:, :half_count]
    slope = (grad_moving * (1.0 - bent_part * bent_part)).astype(jnp.bfloat16)
    grad_cond = grad_cond + narrower(spread_back(slope, kernel))
    kernel_grad = kernel_term(padded, slope)
    if layer_index % 2 == 0:
        joined = jnp.concatenate([grad_cond, grad_moving], axis=1)
    else:
        joined = jnp.concatenate([grad_moving, grad_cond], axis=1)
    return joined, kernel_grad


def run_flow(current, kernels):
    stored_list = []
    for layer_index in range(kernels.shape[0]):
        current, stored = couple(current, kernels[layer_index], layer_index, wrap_both)
        stored_list.append(stored)
    return current, stored_list


def back_flow(gradient, kernels, stored_list):
    grads_list = [None] * kernels.shape[0]
    for layer_index in reversed(range(kernels.shape[0])):
        gradient, kernel_grad = uncouple(gradient, kernels[layer_index], layer_index, stored_list[layer_index], fold_wrap)
        grads_list[layer_index] = kernel_grad
    return gradient, jnp.stack(grads_list)


def pool_field(current, channel_count):
    lattice_count, _, row_count, col_count = current.shape
    return 0.5 * current[:, :channel_count].reshape(lattice_count, channel_count, row_count // 2, 2, col_count // 2, 2).sum(axis=(3, 5))


def unpool_field(gradient):
    return 0.5 * jnp.repeat(jnp.repeat(gradient, 2, axis=2), 2, axis=3)


def reference(lattice_field, fine_kernels, coarse_kernels):
    site_count = lattice_field.shape[2] * lattice_field.shape[3]
    latent, fine_stored = run_flow(lattice_field.astype(jnp.float32), fine_kernels)
    pooled = pool_field(latent, CC)
    coarse_out, coarse_stored = run_flow(pooled, coarse_kernels)
    density = 0.5 * (jnp.sum(latent * latent, axis=(1, 2, 3)) - jnp.sum(pooled * pooled, axis=(1, 2, 3)) + jnp.sum(coarse_out * coarse_out, axis=(1, 2, 3))) / site_count
    pooled_grad, coarse_grads = back_flow(coarse_out / site_count, coarse_kernels, coarse_stored)
    pooled_grad = pooled_grad - pooled / site_count
    fine_start = (latent / site_count).at[:, :CC].add(unpool_field(pooled_grad))
    _, fine_grads = back_flow(fine_start, fine_kernels, fine_stored)
    return latent, coarse_out, density, fine_grads, coarse_grads
```

```python
import functools

import jax
import jax.numpy as jnp
from jax import lax
from jax.experimental import pallas as pl
from jax.experimental.pallas import tpu as pltpu

MESH = pl.DeviceIdType.MESH
F32 = jnp.float32
BF16 = jnp.bfloat16
LANES = 128


def round_up(value, step):
    return -(-value // step) * step


def product(left, right):
    return jnp.dot(left, right, preferred_element_type=F32)


def product_nt(left, right):
    return lax.dot_general(
        left, right, (((1,), (1,)), ((), ())), preferred_element_type=F32
    )


def columns_forward(rows):
    width = rows.shape[1]
    return jnp.concatenate(
        [pltpu.roll(rows, 1, 1), rows, pltpu.roll(rows, width - 1, 1)], axis=0
    )


def columns_backward(rows):
    width = rows.shape[1]
    return jnp.concatenate(
        [pltpu.roll(rows, width - 1, 1), rows, pltpu.roll(rows, 1, 1)], axis=0
    )


def split_product(value, matrix):
    count = value.shape[0]
    first = value.astype(BF16)
    rest = value - first.astype(F32)
    second = rest.astype(BF16)
    third = (rest - second.astype(F32)).astype(BF16)
    stacked = product(jnp.concatenate([first, second, third], axis=0), matrix)
    return stacked[:count] + stacked[count : 2 * count] + stacked[2 * count :]


def pool_columns(value):
    count, width = value.shape
    blocks = width // 256
    stacked = jnp.concatenate(
        [value[:, 256 * b : 256 * (b + 1)] for b in range(blocks)], axis=0
    )
    source = lax.broadcasted_iota(jnp.int32, (256, 128), 0)
    target = lax.broadcasted_iota(jnp.int32, (256, 128), 1)
    matrix = jnp.where((source >> 1) == target, 0.5, 0.0).astype(BF16)
    summed = split_product(stacked, matrix)
    return jnp.concatenate(
        [summed[count * b : count * (b + 1)] for b in range(blocks)], axis=1
    )


def unpool_columns(value):
    count, width = value.shape
    blocks = width // 128
    stacked = jnp.concatenate(
        [value[:, 128 * b : 128 * (b + 1)] for b in range(blocks)], axis=0
    )
    source = lax.broadcasted_iota(jnp.int32, (128, 256), 0)
    target = lax.broadcasted_iota(jnp.int32, (128, 256), 1)
    matrix = jnp.where((target >> 1) == source, 0.5, 0.0).astype(BF16)
    spread = split_product(stacked, matrix)
    return jnp.concatenate(
        [spread[count * b : count * (b + 1)] for b in range(blocks)], axis=1
    )


def flow_kernel(
    slabs, shards, window, own_fine, own_coarse, site_count,
    x_ref, wa_ref, wb_ref,
    lat_ref, coarse_ref, dens_ref, ga_ref, gb_ref,
    wa_buf, wb_buf, halo0, halo1, c1_ref, tiles0, tiles1, tilesb,
    bend0, bend1, pool_buf, slope_ref, shalo,
    sa_ref, sb_ref, ra_buf, rb_buf, aa_buf, ab_buf,
    send_sem, recv_sem,
):
    half = x_ref.shape[1] // 2
    deep = wb_ref.shape[0] - 2 * half
    mc = deep // 4
    cc = 2 * mc
    patch = 9 * half
    three = 3 * half
    cpatch = 9 * mc
    inverse = 1.0 / site_count
    me = lax.axis_index("slab")
    mine = lax.axis_index("dp")
    above = lax.rem(me + slabs - 1, slabs)
    below = lax.rem(me + 1, slabs)

    barrier = pltpu.get_barrier_semaphore()
    for step in range(1, slabs):
        pl.semaphore_signal(
            barrier, inc=1, device_id={"slab": lax.rem(me + step, slabs)}, device_id_type=MESH
        )
    for step in range(1, shards):
        pl.semaphore_signal(
            barrier, inc=1, device_id={"dp": lax.rem(mine + step, shards)}, device_id_type=MESH
        )
    pl.semaphore_wait(barrier, slabs + shards - 2)

    used = [0]
    started = []

    def send(source, target, device):
        index = used[0]
        used[0] += 1
        copy = pltpu.make_async_remote_copy(
            src_ref=source,
            dst_ref=target,
            send_sem=send_sem.at[index],
            recv_sem=recv_sem.at[index],
            device_id=device,
            device_id_type=MESH,
        )
        copy.start()
        started.append(copy)
        return copy

    wa_copies, wb_copies = [], []
    for step in range(1, shards):
        peer = lax.rem(mine + step, shards)
        wa_copies.append(send(wa_ref, wa_buf.at[step - 1], {"dp": peer}))
    from_above = send(x_ref.at[1, 0:half], halo0.at[0], {"slab": below})
    from_below = send(x_ref.at[0, 0:half], halo0.at[1], {"slab": above})
    for step in range(1, shards):
        peer = lax.rem(mine + step, shards)
        wb_copies.append(send(wb_ref, wb_buf.at[step - 1], {"dp": peer}))

    sa_ref[...] = jnp.zeros_like(sa_ref)
    sb_ref[...] = jnp.zeros_like(sb_ref)

    def set_tile(tiles, index, rows, turn):
        tiles[three * index : three * (index + 1), :] = turn(rows).astype(BF16)

    for i in range(2):
        set_tile(tiles0, i + 1, x_ref[i, 0:half].astype(F32), columns_forward)
    total = wa_ref[...].astype(F32)
    for step in range(1, shards):
        wa_copies[step - 1].wait_recv()
        total = total + wa_buf[step - 1].astype(F32)
    weight0 = total[:, 0:patch].astype(BF16)
    from_above.wait_recv()
    set_tile(tiles0, 0, halo0[0].astype(F32), columns_forward)
    from_below.wait_recv()
    set_tile(tiles0, 3, halo0[1].astype(F32), columns_forward)
    density = jnp.zeros((half, x_ref.shape[2]), F32)
    for i in range(2):
        bent = jnp.tanh(product(weight0, tiles0[three * i : three * i + patch, :]))
        moved = x_ref[i, half:].astype(F32) + bent
        lat_ref[i, half:] = moved
        bend0[i] = 1.0 - bent * bent
        c1_ref[i] = moved.astype(BF16)
    from_above = send(c1_ref.at[1], halo1.at[0], {"slab": below})
    from_below = send(c1_ref.at[0], halo1.at[1], {"slab": above})

    for i in range(2):
        set_tile(tiles1, i + 1, c1_ref[i].astype(F32), columns_forward)
        moved = lat_ref[i, half:]
        density = density + moved * moved
    total = wb_ref[...].astype(F32)
    for step in range(1, shards):
        wb_copies[step - 1].wait_recv()
        total = total + wb_buf[step - 1].astype(F32)
    weights = total.astype(BF16)
    weight1 = weights[0:half, 0:patch]
    back1 = weights[half : 2 * half, 0:patch]
    coarse_weights = total[2 * half :, 0:cpatch]
    cfor0, cfor1, cback1, cback0 = [
        coarse_weights[mc * k : mc * (k + 1)].astype(BF16) for k in range(4)
    ]
    from_above.wait_recv()
    set_tile(tiles1, 0, halo1[0].astype(F32), columns_forward)
    from_below.wait_recv()
    set_tile(tiles1, 3, halo1[1].astype(F32), columns_forward)
    for i in range(2):
        bent = jnp.tanh(product(weight1, tiles1[three * i : three * i + patch, :]))
        moved = x_ref[i, 0:half].astype(F32) + bent
        lat_ref[i, 0:half] = moved
        bend1[i] = 1.0 - bent * bent
        density = density + moved * moved

    pool_buf[0] = pool_columns(lat_ref[0, 0:cc] + lat_ref[1, 0:cc])
    pool_copies = []
    for k in range(1, window):
        offset = k if k <= window // 2 else k - window
        peer = lax.rem(me - offset + slabs, slabs)
        pool_copies.append(send(pool_buf.at[0], pool_buf.at[k], {"slab": peer}))
    for i in range(2):
        slope_ref[i, cc:half] = (lat_ref[i, cc:half] * inverse * bend1[i, cc:half]).astype(BF16)
    high_above = send(slope_ref.at[1, cc:half], shalo.at[0, cc:half], {"slab": below})
    high_below = send(slope_ref.at[0, cc:half], shalo.at[1, cc:half], {"slab": above})
    for copy in pool_copies:
        copy.wait_recv()

    width = pool_buf.shape[2]

    def coarse_patches(rows, turn, sign, wanted):
        turned = [turn(row) for row in rows]
        columns = []
        for k in wanted:
            near = [turned[(k + sign * (p - 1)) % window] for p in range(3)]
            columns.append(jnp.concatenate(near, axis=0))
        return jnp.concatenate(columns, axis=1).astype(BF16)

    def cut(value):
        return [value[:, width * k : width * (k + 1)] for k in range(value.shape[1] // width)]

    def rounded(value):
        return value.astype(BF16).astype(F32)

    everything = range(window)
    low = jnp.concatenate([pool_buf[k, 0:mc] for k in everything], axis=1)
    high = jnp.concatenate([pool_buf[k, mc:cc] for k in everything], axis=1)
    patches0 = coarse_patches(cut(rounded(low)), columns_forward, 1, everything)
    bent_c0 = jnp.tanh(product(cfor0, patches0))
    high = high + bent_c0
    patches1 = coarse_patches(cut(rounded(high)), columns_forward, 1, everything)
    bent_c1 = jnp.tanh(product(cfor1, patches1))
    low = low + bent_c1
    coarse_own = jnp.concatenate([low[:, 0:width], high[:, 0:width]], axis=0)
    coarse_ref[...] = coarse_own
    pooled = pool_buf[0]

    grad_low = low * inverse
    slope_c1 = (grad_low * (1.0 - bent_c1 * bent_c1)).astype(BF16)
    kernel_c1 = product_nt(slope_c1[:, 0:width], patches1[:, 0:width])
    back_patches = coarse_patches(cut(slope_c1.astype(F32)), columns_backward, -1, everything)
    grad_high = high * inverse + product(cback1, back_patches)
    slope_c0 = (grad_high * (1.0 - bent_c0 * bent_c0)).astype(BF16)
    kernel_c0 = product_nt(slope_c0[:, 0:width], patches0[:, 0:width])
    back_patches = coarse_patches(cut(slope_c0.astype(F32)), columns_backward, -1, [0])
    grad_own = grad_low[:, 0:width] + product(cback0, back_patches)
    pooled_grad = jnp.concatenate([grad_own, grad_high[:, 0:width]], axis=0) - pooled * inverse
    spread = unpool_columns(pooled_grad)

    for i in range(2):
        slope_ref[i, 0:cc] = ((lat_ref[i, 0:cc] * inverse + spread) * bend1[i, 0:cc]).astype(BF16)
    low_above = send(slope_ref.at[1, 0:cc], shalo.at[0, 0:cc], {"slab": below})
    low_below = send(slope_ref.at[0, 0:cc], shalo.at[1, 0:cc], {"slab": above})
    kernel_1 = product_nt(slope_ref[0], tiles1[0:patch, :])
    kernel_1 = kernel_1 + product_nt(slope_ref[1], tiles1[three : three + patch, :])
    pad_fine = round_up(own_fine, 8)
    for d in range(shards):
        sb_ref[d, 0:own_fine, 0:patch] = kernel_1[own_fine * d : own_fine * (d + 1)]
        sb_ref[d, pad_fine : pad_fine + own_coarse, 0:cpatch] = kernel_c0[
            own_coarse * d : own_coarse * (d + 1)
        ]
        sb_ref[d, pad_fine + own_coarse : pad_fine + 2 * own_coarse, 0:cpatch] = kernel_c1[
            own_coarse * d : own_coarse * (d + 1)
        ]
    rb_copies = []
    for step in range(1, shards):
        peer = lax.rem(mine + step, shards)
        rb_copies.append(send(sb_ref.at[peer], rb_buf.at[step - 1], {"dp": peer}))
    for i in range(2):
        set_tile(tilesb, 2 - i, slope_ref[i].astype(F32), columns_backward)

    folded = density[0:8]
    for b in range(1, half // 8):
        folded = folded + density[8 * b : 8 * (b + 1)]
    narrow = folded[:, 0:width] + folded[:, width:]
    for b in range(cc // 8):
        part = slice(8 * b, 8 * (b + 1))
        narrow = narrow - pooled[part] * pooled[part] + coarse_own[part] * coarse_own[part]
    tile = narrow[:, 0:LANES]
    for b in range(1, width // LANES):
        tile = tile + narrow[:, LANES * b : LANES * (b + 1)]
    tile = tile * (0.5 * inverse)

    high_above.wait_recv()
    low_above.wait_recv()
    set_tile(tilesb, 3, shalo[0].astype(F32), columns_backward)
    high_below.wait_recv()
    low_below.wait_recv()
    set_tile(tilesb, 0, shalo[1].astype(F32), columns_backward)
    kernel_0 = None
    for i in range(2):
        start = three * (1 - i)
        grad = lat_ref[i, half:] * inverse + product(back1, tilesb[start : start + patch, :])
        slope = (grad * bend0[i]).astype(BF16)
        term = product_nt(slope, tiles0[three * i : three * i + patch, :])
        kernel_0 = term if kernel_0 is None else kernel_0 + term
    for d in range(shards):
        sa_ref[d, 0:own_fine, 0:patch] = kernel_0[own_fine * d : own_fine * (d + 1)]
    ra_copies = []
    for step in range(1, shards):
        peer = lax.rem(mine + step, shards)
        ra_copies.append(send(sa_ref.at[peer], ra_buf.at[step - 1], {"dp": peer}))

    def over_slabs(gathered):
        copies = []
        for step in range(1, slabs):
            peer = lax.rem(me + step, slabs)
            copies.append(used[0])
            send(gathered.at[me], gathered.at[me], {"slab": peer})
        return copies

    block = sb_ref[mine]
    for step in range(1, shards):
        rb_copies[step - 1].wait_recv()
        block = block + rb_buf[step - 1]
    rows_b = sb_ref.shape[1]
    ab_buf[me, 0:rows_b] = block
    ab_buf[me, rows_b:] = jnp.concatenate(
        [tile, jnp.zeros((8, ab_buf.shape[2] - LANES), F32)], axis=1
    )
    ab_copies = over_slabs(ab_buf)
    block = sa_ref[mine]
    for step in range(1, shards):
        ra_copies[step - 1].wait_recv()
        block = block + ra_buf[step - 1]
    aa_buf[me] = block
    aa_copies = over_slabs(aa_buf)

    def wait_slabs(gathered, copies):
        for step in range(1, slabs):
            source = lax.rem(me - step + slabs, slabs)
            pltpu.make_async_remote_copy(
                src_ref=gathered.at[me],
                dst_ref=gathered.at[source],
                send_sem=send_sem.at[copies[step - 1]],
                recv_sem=recv_sem.at[copies[step - 1]],
                device_id={"slab": source},
                device_id_type=MESH,
            ).wait_recv()

    wait_slabs(ab_buf, ab_copies)
    block = ab_buf[0]
    for s in range(1, slabs):
        block = block + ab_buf[s]
    gb_ref[...] = block[0:rows_b]
    dens_ref[...] = jnp.broadcast_to(jnp.sum(block[rows_b:, 0:LANES], keepdims=True), (8, LANES))
    wait_slabs(aa_buf, aa_copies)
    block = aa_buf[0]
    for s in range(1, slabs):
        block = block + aa_buf[s]
    ga_ref[...] = block
    for copy in started:
        copy.wait_send()


def on_device(lattice_field, fine_kernels, coarse_kernels):
    slabs, shards = lax.axis_size("slab"), lax.axis_size("dp")
    mine = lax.axis_index("dp")
    _, channels, height, cols = lattice_field.shape
    _, own_fine, half, _, _ = fine_kernels.shape
    _, own_coarse, mc, _, _ = coarse_kernels.shape
    cc, width = 2 * mc, cols // 2
    patch, cpatch = 9 * half, 9 * mc
    padded = round_up(patch, LANES)
    site_count = height * slabs * cols
    window = min(slabs, 9)

    def embedded(kernel, own):
        count = own * shards
        tiled = jnp.tile(kernel, (1, shards, 1, 1, 1))
        owner = lax.broadcasted_iota(jnp.int32, (1, count, 1, 1, 1), 1) // own
        full = jnp.where(owner == mine, tiled, jnp.zeros_like(tiled))
        forward = jnp.transpose(full, (0, 1, 3, 4, 2)).reshape(2, count, -1)
        backward = jnp.transpose(full, (0, 2, 3, 4, 1)).reshape(2, count, -1)
        pads = ((0, 0), (0, 0), (0, padded - forward.shape[2]))
        return jnp.pad(forward, pads), jnp.pad(backward, pads)

    forward, backward = embedded(fine_kernels, own_fine)
    cforward, cbackward = embedded(coarse_kernels, own_coarse)
    wa = forward[0]
    wb = jnp.concatenate(
        [forward[1], backward[1], cforward[0], cforward[1], cbackward[1], cbackward[0]], axis=0
    )
    x = jnp.transpose(lattice_field[0], (1, 0, 2))

    pad_fine = round_up(own_fine, 8)
    rows_b = pad_fine + 8
    copies = 4 * (shards - 1) + 8 + (window - 1) + 2 * (slabs - 1)
    vmem = pl.BlockSpec(memory_space=pltpu.VMEM)
    lat, coarse, dens, ga, gb = pl.pallas_call(
        functools.partial(
            flow_kernel, slabs, shards, window, own_fine, own_coarse, site_count
        ),
        out_shape=(
            jax.ShapeDtypeStruct((2, channels, cols), F32),
            jax.ShapeDtypeStruct((cc, width), F32),
            jax.ShapeDtypeStruct((8, LANES), F32),
            jax.ShapeDtypeStruct((pad_fine, padded), F32),
            jax.ShapeDtypeStruct((rows_b, padded), F32),
        ),
        in_specs=[vmem] * 3,
        out_specs=(vmem,) * 5,
        scratch_shapes=[
            pltpu.VMEM((shards - 1,) + wa.shape, BF16),
            pltpu.VMEM((shards - 1,) + wb.shape, BF16),
            pltpu.VMEM((2, half, cols), BF16),
            pltpu.VMEM((2, half, cols), BF16),
            pltpu.VMEM((2, half, cols), BF16),
            pltpu.VMEM((12 * half, cols), BF16),
            pltpu.VMEM((12 * half, cols), BF16),
            pltpu.VMEM((12 * half, cols), BF16),
            pltpu.VMEM((2, half, cols), F32),
            pltpu.VMEM((2, half, cols), F32),
            pltpu.VMEM((window, cc, width), F32),
            pltpu.VMEM((2, half, cols), BF16),
            pltpu.VMEM((2, half, cols), BF16),
            pltpu.VMEM((shards, pad_fine, padded), F32),
            pltpu.VMEM((shards, rows_b, padded), F32),
            pltpu.VMEM((shards - 1, pad_fine, padded), F32),
            pltpu.VMEM((shards - 1, rows_b, padded), F32),
            pltpu.VMEM((slabs, pad_fine, padded), F32),
            pltpu.VMEM((slabs, rows_b + 8, padded), F32),
            pltpu.SemaphoreType.DMA((copies,)),
            pltpu.SemaphoreType.DMA((copies,)),
        ],
        compiler_params=pltpu.CompilerParams(
            collective_id=0, has_side_effects=True, vmem_limit_bytes=40 * 1024 * 1024
        ),
    )(x, wa, wb)

    def unfold(rows, own, count):
        return jnp.transpose(rows.reshape(own, 3, 3, count), (0, 3, 1, 2))

    fine = jnp.stack(
        [
            unfold(ga[0:own_fine, 0:patch], own_fine, half),
            unfold(gb[0:own_fine, 0:patch], own_fine, half),
        ]
    )
    coarse_rows = gb[pad_fine : pad_fine + 2 * own_coarse, 0:cpatch]
    coarse_grads = jnp.stack(
        [
            unfold(coarse_rows[0:own_coarse], own_coarse, mc),
            unfold(coarse_rows[own_coarse:], own_coarse, mc),
        ]
    )
    return (
        jnp.transpose(lat, (1, 0, 2))[None],
        coarse[None, :, None, :],
        dens[0, 0:1],
        fine,
        coarse_grads,
    )


def solution(mesh):
    from jax.sharding import PartitionSpec as P

    in_specs = (
        P(("groups", "dp"), None, "slab", None),
        P(None, "dp", None, None, None),
        P(None, "dp", None, None, None),
    )
    out_specs = (
        P(("groups", "dp"), None, "slab", None),
        P(("groups", "dp"), None, "slab", None),
        P(("groups", "dp")),
        P("groups", "dp", None, None, None),
        P("groups", "dp", None, None, None),
    )
    return jax.shard_map(
        on_device, mesh=mesh, in_specs=in_specs, out_specs=out_specs, check_vma=False
    )
```

```python
import functools

import jax
import jax.numpy as jnp
from jax import lax
from jax.experimental import pallas as pl
from jax.experimental.pallas import tpu as pltpu

MESH = pl.DeviceIdType.MESH
F32 = jnp.float32
BF16 = jnp.bfloat16
LANES = 128


def round_up(value, step):
    return -(-value // step) * step


def product(left, right):
    return jnp.dot(left, right, preferred_element_type=F32)


def product_nt(left, right):
    return lax.dot_general(
        left, right, (((1,), (1,)), ((), ())), preferred_element_type=F32
    )


def columns_forward(rows):
    width = rows.shape[1]
    return jnp.concatenate(
        [pltpu.roll(rows, 1, 1), rows, pltpu.roll(rows, width - 1, 1)], axis=0
    )


def columns_backward(rows):
    width = rows.shape[1]
    return jnp.concatenate(
        [pltpu.roll(rows, width - 1, 1), rows, pltpu.roll(rows, 1, 1)], axis=0
    )


def split_product(value, matrix):
    count = value.shape[0]
    first = value.astype(BF16)
    rest = value - first.astype(F32)
    second = rest.astype(BF16)
    third = (rest - second.astype(F32)).astype(BF16)
    stacked = product(jnp.concatenate([first, second, third], axis=0), matrix)
    return stacked[:count] + stacked[count : 2 * count] + stacked[2 * count :]


def pool_columns(value):
    count, width = value.shape
    blocks = width // 256
    stacked = jnp.concatenate(
        [value[:, 256 * b : 256 * (b + 1)] for b in range(blocks)], axis=0
    )
    source = lax.broadcasted_iota(jnp.int32, (256, 128), 0)
    target = lax.broadcasted_iota(jnp.int32, (256, 128), 1)
    matrix = jnp.where((source >> 1) == target, 0.5, 0.0).astype(BF16)
    summed = split_product(stacked, matrix)
    return jnp.concatenate(
        [summed[count * b : count * (b + 1)] for b in range(blocks)], axis=1
    )


def unpool_columns(value):
    count, width = value.shape
    blocks = width // 128
    stacked = jnp.concatenate(
        [value[:, 128 * b : 128 * (b + 1)] for b in range(blocks)], axis=0
    )
    source = lax.broadcasted_iota(jnp.int32, (128, 256), 0)
    target = lax.broadcasted_iota(jnp.int32, (128, 256), 1)
    matrix = jnp.where((target >> 1) == source, 0.5, 0.0).astype(BF16)
    spread = split_product(stacked, matrix)
    return jnp.concatenate(
        [spread[count * b : count * (b + 1)] for b in range(blocks)], axis=1
    )


def flow_kernel(
    slabs, shards, window, own_fine, own_coarse, site_count,
    x_ref, wa_ref, wb_ref,
    out_ref, coarse_ref, dens_ref, fine_ref, cgrad_ref,
    wa_buf, wb_buf, halo0, halo1, c1_ref, tiles0, tiles1, tilesb,
    lat_ref, bend0, bend1, pool_buf, slope_ref, shalo,
    sa_ref, sb_ref, ra_buf, rb_buf, aa_buf, ab_buf,
    send_sem, recv_sem,
):
    half = x_ref.shape[1] // 2
    deep = wb_ref.shape[0] - 2 * half
    mc = deep // 4
    cc = 2 * mc
    patch = 9 * half
    three = 3 * half
    cpatch = 9 * mc
    tail = patch // LANES * LANES
    inset = patch - tail
    inverse = 1.0 / site_count
    me = lax.axis_index("slab")
    mine = lax.axis_index("dp")
    above = lax.rem(me + slabs - 1, slabs)
    below = lax.rem(me + 1, slabs)

    barrier = pltpu.get_barrier_semaphore()
    for step in range(1, slabs):
        pl.semaphore_signal(
            barrier, inc=1, device_id={"slab": lax.rem(me + step, slabs)}, device_id_type=MESH
        )
    for step in range(1, shards):
        pl.semaphore_signal(
            barrier, inc=1, device_id={"dp": lax.rem(mine + step, shards)}, device_id_type=MESH
        )
    pl.semaphore_wait(barrier, slabs + shards - 2)

    used = [0]
    started = []

    def send(source, target, device):
        index = used[0]
        used[0] += 1
        copy = pltpu.make_async_remote_copy(
            src_ref=source,
            dst_ref=target,
            send_sem=send_sem.at[index],
            recv_sem=recv_sem.at[index],
            device_id=device,
            device_id_type=MESH,
        )
        copy.start()
        started.append(copy)
        return copy

    wa_copies, wb_copies = [], []
    for step in range(1, shards):
        peer = lax.rem(mine + step, shards)
        wa_copies.append(send(wa_ref, wa_buf.at[step - 1], {"dp": peer}))
    from_above = send(x_ref.at[1, 0:half], halo0.at[0], {"slab": below})
    from_below = send(x_ref.at[0, 0:half], halo0.at[1], {"slab": above})
    for step in range(1, shards):
        peer = lax.rem(mine + step, shards)
        wb_copies.append(send(wb_ref, wb_buf.at[step - 1], {"dp": peer}))

    sa_ref[...] = jnp.zeros_like(sa_ref)
    sb_ref[...] = jnp.zeros_like(sb_ref)

    def set_tile(tiles, index, rows, turn):
        tiles[three * index : three * (index + 1), :] = turn(rows).astype(BF16)

    def own_terms(weight, tiles, first, second):
        stacked = jnp.concatenate(
            [weight[:, first : first + 2 * three], weight[:, second : second + 2 * three]], axis=0
        ).astype(BF16)
        both = product(stacked, tiles[three : 3 * three, :])
        return both[0:half], both[half:]

    for i in range(2):
        set_tile(tiles0, i + 1, x_ref[i, 0:half].astype(F32), columns_forward)
    total = wa_ref[...].astype(F32)
    for step in range(1, shards):
        wa_copies[step - 1].wait_recv()
        total = total + wa_buf[step - 1].astype(F32)
    sums = own_terms(total, tiles0, three, 0)
    edges = [total[:, 0:three].astype(BF16), total[:, 2 * three : patch].astype(BF16)]
    from_above.wait_recv()
    set_tile(tiles0, 0, halo0[0].astype(F32), columns_forward)
    from_below.wait_recv()
    set_tile(tiles0, 3, halo0[1].astype(F32), columns_forward)
    density = jnp.zeros((half, x_ref.shape[2]), F32)
    for i in range(2):
        edge = three * 3 * i
        bent = jnp.tanh(sums[i] + product(edges[i], tiles0[edge : edge + three, :]))
        moved = x_ref[i, half:].astype(F32) + bent
        c1_ref[i] = moved.astype(BF16)
        lat_ref[i, half:] = moved
        bend0[i] = 1.0 - bent * bent
    from_above = send(c1_ref.at[1], halo1.at[0], {"slab": below})
    from_below = send(c1_ref.at[0], halo1.at[1], {"slab": above})

    for i in range(2):
        set_tile(tiles1, i + 1, c1_ref[i].astype(F32), columns_forward)
        moved = lat_ref[i, half:]
        density = density + moved * moved
    total = wb_ref[...].astype(F32)
    for step in range(1, shards):
        wb_copies[step - 1].wait_recv()
        total = total + wb_buf[step - 1].astype(F32)
    weight1 = total[0:half]
    back1 = total[half : 2 * half]
    sums = own_terms(weight1, tiles1, three, 0)
    edges = [weight1[:, 0:three].astype(BF16), weight1[:, 2 * three : patch].astype(BF16)]
    coarse_weights = total[2 * half :, 0:cpatch]
    cfor0, cfor1, cback1, cback0 = [
        coarse_weights[mc * k : mc * (k + 1)].astype(BF16) for k in range(4)
    ]
    from_above.wait_recv()
    set_tile(tiles1, 0, halo1[0].astype(F32), columns_forward)
    from_below.wait_recv()
    set_tile(tiles1, 3, halo1[1].astype(F32), columns_forward)
    sums = [
        sums[i] + product(edges[i], tiles1[three * 3 * i : three * (3 * i + 1), :])
        for i in range(2)
    ]

    def finish(part):
        for i in range(2):
            bent = jnp.tanh(sums[i][part])
            lat_ref[i, part] = x_ref[i, part].astype(F32) + bent
            bend1[i, part] = 1.0 - bent * bent

    finish(slice(0, cc))

    pool_buf[0] = pool_columns(lat_ref[0, 0:cc] + lat_ref[1, 0:cc])
    pool_copies = []
    for k in range(1, window):
        offset = k if k <= window // 2 else k - window
        peer = lax.rem(me - offset + slabs, slabs)
        pool_copies.append(send(pool_buf.at[0], pool_buf.at[k], {"slab": peer}))
    finish(slice(cc, half))
    for i in range(2):
        slope_ref[i, cc:half] = (lat_ref[i, cc:half] * inverse * bend1[i, cc:half]).astype(BF16)
    high_above = send(slope_ref.at[1, cc:half], shalo.at[0, cc:half], {"slab": below})
    high_below = send(slope_ref.at[0, cc:half], shalo.at[1, cc:half], {"slab": above})
    tiles = x_ref.shape[2] // LANES
    for i in range(2):
        moved = lat_ref[i, 0:half]
        density = density + moved * moved
        for b in range(tiles):
            out_ref[pl.ds(2 * b + i, 2 * half, stride=2 * tiles), :] = lat_ref[
                i, :, LANES * b : LANES * (b + 1)
            ]
    for copy in pool_copies:
        copy.wait_recv()

    width = pool_buf.shape[2]

    def coarse_patches(rows, turn, sign, wanted):
        turned = [turn(row) for row in rows]
        columns = []
        for k in wanted:
            near = [turned[(k + sign * (p - 1)) % window] for p in range(3)]
            columns.append(jnp.concatenate(near, axis=0))
        return jnp.concatenate(columns, axis=1)

    def cut(value):
        return [value[:, width * k : width * (k + 1)] for k in range(value.shape[1] // width)]

    def rounded(value):
        return value.astype(BF16).astype(F32)

    everything = range(window)
    low = jnp.concatenate([pool_buf[k, 0:mc] for k in everything], axis=1)
    high = jnp.concatenate([pool_buf[k, mc:cc] for k in everything], axis=1)
    patches0 = coarse_patches(cut(rounded(low)), columns_forward, 1, everything)
    bent_c0 = jnp.tanh(product(cfor0, patches0.astype(BF16)))
    high = high + bent_c0
    patches1 = coarse_patches(cut(rounded(high)), columns_forward, 1, everything)
    bent_c1 = jnp.tanh(product(cfor1, patches1.astype(BF16)))
    low = low + bent_c1
    coarse_own = jnp.concatenate([low[:, 0:width], high[:, 0:width]], axis=0)
    for b in range(width // LANES):
        coarse_ref[pl.ds(b, cc, stride=width // LANES), :] = coarse_own[
            :, LANES * b : LANES * (b + 1)
        ]
    pooled = pool_buf[0]

    def coarse_kernel_grad(slope, patches):
        widened = jnp.concatenate(
            [
                jnp.zeros((inset, width), F32),
                patches[:, 0:width],
                jnp.zeros((LANES - inset - cpatch, width), F32),
            ],
            axis=0,
        )
        return product_nt(slope[:, 0:width], widened.astype(BF16))

    grad_low = low * inverse
    slope_c1 = (grad_low * (1.0 - bent_c1 * bent_c1)).astype(BF16)
    kernel_c1 = coarse_kernel_grad(slope_c1, patches1)
    back_patches = coarse_patches(cut(slope_c1.astype(F32)), columns_backward, -1, everything)
    grad_high = high * inverse + product(cback1, back_patches.astype(BF16))
    slope_c0 = (grad_high * (1.0 - bent_c0 * bent_c0)).astype(BF16)
    kernel_c0 = coarse_kernel_grad(slope_c0, patches0)
    back_patches = coarse_patches(cut(slope_c0.astype(F32)), columns_backward, -1, [0])
    grad_own = grad_low[:, 0:width] + product(cback0, back_patches.astype(BF16))
    pooled_grad = jnp.concatenate([grad_own, grad_high[:, 0:width]], axis=0) - pooled * inverse
    spread = unpool_columns(pooled_grad)

    for i in range(2):
        slope_ref[i, 0:cc] = ((lat_ref[i, 0:cc] * inverse + spread) * bend1[i, 0:cc]).astype(BF16)
    low_above = send(slope_ref.at[1, 0:cc], shalo.at[0, 0:cc], {"slab": below})
    low_below = send(slope_ref.at[0, 0:cc], shalo.at[1, 0:cc], {"slab": above})
    kernel_1 = product_nt(slope_ref[0], tiles1[0:patch, :])
    kernel_1 = kernel_1 + product_nt(slope_ref[1], tiles1[three : three + patch, :])
    for d in range(shards):
        sb_ref[d, 0:own_fine, 0:patch] = kernel_1[own_fine * d : own_fine * (d + 1)]
        for l, kernel_c in enumerate((kernel_c0, kernel_c1)):
            place = slice(own_coarse * l, own_coarse * (l + 1))
            sb_ref[d, place, tail:] = (
                sb_ref[d, place, tail:] + kernel_c[own_coarse * d : own_coarse * (d + 1)]
            )
    rb_copies = []
    for step in range(1, shards):
        peer = lax.rem(mine + step, shards)
        rb_copies.append(send(sb_ref.at[peer], rb_buf.at[step - 1], {"dp": peer}))
    for i in range(2):
        set_tile(tilesb, 2 - i, slope_ref[i].astype(F32), columns_backward)

    folded = density[0:8]
    for b in range(1, half // 8):
        folded = folded + density[8 * b : 8 * (b + 1)]
    narrow = folded[:, 0:width] + folded[:, width:]
    for b in range(cc // 8):
        part = slice(8 * b, 8 * (b + 1))
        narrow = narrow - pooled[part] * pooled[part] + coarse_own[part] * coarse_own[part]
    tile = narrow[:, 0:LANES]
    for b in range(1, width // LANES):
        tile = tile + narrow[:, LANES * b : LANES * (b + 1)]
    site_density = jnp.sum(tile * (0.5 * inverse), keepdims=True)
    sums = own_terms(back1, tilesb, 0, three)
    edges = [back1[:, 2 * three : patch].astype(BF16), back1[:, 0:three].astype(BF16)]

    high_above.wait_recv()
    low_above.wait_recv()
    set_tile(tilesb, 3, shalo[0].astype(F32), columns_backward)
    high_below.wait_recv()
    low_below.wait_recv()
    set_tile(tilesb, 0, shalo[1].astype(F32), columns_backward)
    kernel_0 = None
    for i in range(2):
        edge = three * 3 * (1 - i)
        grad = (
            lat_ref[i, half:] * inverse
            + sums[i]
            + product(edges[i], tilesb[edge : edge + three, :])
        )
        slope = (grad * bend0[i]).astype(BF16)
        term = product_nt(slope, tiles0[three * i : three * i + patch, :])
        kernel_0 = term if kernel_0 is None else kernel_0 + term
    for d in range(shards):
        sa_ref[d, 0:own_fine, 0:patch] = kernel_0[own_fine * d : own_fine * (d + 1)]
    ra_copies = []
    for step in range(1, shards):
        peer = lax.rem(mine + step, shards)
        ra_copies.append(send(sa_ref.at[peer], ra_buf.at[step - 1], {"dp": peer}))

    def over_slabs(gathered):
        copies = []
        for step in range(1, slabs):
            peer = lax.rem(me + step, slabs)
            copies.append(used[0])
            send(gathered.at[me], gathered.at[me], {"slab": peer})
        return copies

    block = sb_ref[mine]
    for step in range(1, shards):
        rb_copies[step - 1].wait_recv()
        block = block + rb_buf[step - 1]
    row = lax.broadcasted_iota(jnp.int32, block.shape, 0)
    lane = lax.broadcasted_iota(jnp.int32, block.shape, 1)
    ab_buf[me] = jnp.where((row == 2 * own_coarse) & (lane == patch), site_density, block)
    ab_copies = over_slabs(ab_buf)
    block = sa_ref[mine]
    for step in range(1, shards):
        ra_copies[step - 1].wait_recv()
        block = block + ra_buf[step - 1]
    aa_buf[me] = block
    aa_copies = over_slabs(aa_buf)

    def wait_slabs(gathered, copies):
        for step in range(1, slabs):
            source = lax.rem(me - step + slabs, slabs)
            pltpu.make_async_remote_copy(
                src_ref=gathered.at[me],
                dst_ref=gathered.at[source],
                send_sem=send_sem.at[copies[step - 1]],
                recv_sem=recv_sem.at[copies[step - 1]],
                device_id={"slab": source},
                device_id_type=MESH,
            ).wait_recv()

    wait_slabs(ab_buf, ab_copies)
    block = ab_buf[0]
    for s in range(1, slabs):
        block = block + ab_buf[s]
    dens_ref[...] = block[2 * own_coarse : 2 * own_coarse + 1, patch : patch + 1]
    for k in range(9):
        fine_ref[1, k] = block[0:own_fine, half * k : half * (k + 1)]
        for l in range(2):
            cgrad_ref[l, k] = block[
                own_coarse * l : own_coarse * (l + 1), patch + mc * k : patch + mc * (k + 1)
            ]
    wait_slabs(aa_buf, aa_copies)
    block = aa_buf[0]
    for s in range(1, slabs):
        block = block + aa_buf[s]
    for k in range(9):
        fine_ref[0, k] = block[0:own_fine, half * k : half * (k + 1)]
    for copy in started:
        copy.wait_send()


def store_kernel(*refs):
    sem = refs[-1]
    copies = [pltpu.make_async_copy(refs[k], refs[5 + k], sem.at[k]) for k in range(5)]
    for copy in copies:
        copy.start()
    for copy in copies:
        copy.wait()


def on_device(lattice_field, fine_kernels, coarse_kernels):
    slabs, shards = lax.axis_size("slab"), lax.axis_size("dp")
    mine = lax.axis_index("dp")
    _, channels, height, cols = lattice_field.shape
    _, own_fine, half, _, _ = fine_kernels.shape
    _, own_coarse, mc, _, _ = coarse_kernels.shape
    cc, width = 2 * mc, cols // 2
    patch, cpatch = 9 * half, 9 * mc
    padded = round_up(patch, LANES)
    site_count = height * slabs * cols
    window = min(slabs, 9)

    def embedded(kernel, own):
        count = own * shards
        tiled = jnp.tile(kernel, (1, shards, 1, 1, 1))
        owner = lax.broadcasted_iota(jnp.int32, (1, count, 1, 1, 1), 1) // own
        full = jnp.where(owner == mine, tiled, jnp.zeros_like(tiled))
        forward = jnp.transpose(full, (0, 1, 3, 4, 2)).reshape(2, count, -1)
        backward = jnp.transpose(full, (0, 2, 3, 4, 1)).reshape(2, count, -1)
        pads = ((0, 0), (0, 0), (0, padded - forward.shape[2]))
        return jnp.pad(forward, pads), jnp.pad(backward, pads)

    forward, backward = embedded(fine_kernels, own_fine)
    cforward, cbackward = embedded(coarse_kernels, own_coarse)
    wa = forward[0]
    wb = jnp.concatenate(
        [forward[1], backward[1], cforward[0], cforward[1], cbackward[1], cbackward[0]], axis=0
    )
    x = jnp.transpose(lattice_field[0], (1, 0, 2))

    pad_fine = round_up(own_fine, 8)
    tall = channels * height * cols // LANES
    copies = 4 * (shards - 1) + 8 + (window - 1) + 2 * (slabs - 1)
    vmem = pl.BlockSpec(memory_space=pltpu.VMEM)
    shapes = (
        jax.ShapeDtypeStruct((tall, LANES), F32),
        jax.ShapeDtypeStruct((cc * width // LANES, LANES), F32),
        jax.ShapeDtypeStruct((1, 1), F32),
        jax.ShapeDtypeStruct((2, 9, own_fine, half), F32),
        jax.ShapeDtypeStruct((2, 9, own_coarse, mc), F32),
    )
    results = pl.pallas_call(
        functools.partial(
            flow_kernel, slabs, shards, window, own_fine, own_coarse, site_count
        ),
        out_shape=shapes,
        in_specs=[vmem] * 3,
        out_specs=(vmem,) * 5,
        scratch_shapes=[
            pltpu.VMEM((shards - 1,) + wa.shape, BF16),
            pltpu.VMEM((shards - 1,) + wb.shape, BF16),
            pltpu.VMEM((2, half, cols), BF16),
            pltpu.VMEM((2, half, cols), BF16),
            pltpu.VMEM((2, half, cols), BF16),
            pltpu.VMEM((12 * half, cols), BF16),
            pltpu.VMEM((12 * half, cols), BF16),
            pltpu.VMEM((12 * half, cols), BF16),
            pltpu.VMEM((2, channels, cols), F32),
            pltpu.VMEM((2, half, cols), F32),
            pltpu.VMEM((2, half, cols), F32),
            pltpu.VMEM((window, cc, width), F32),
            pltpu.VMEM((2, half, cols), BF16),
            pltpu.VMEM((2, half, cols), BF16),
            pltpu.VMEM((shards, pad_fine, padded), F32),
            pltpu.VMEM((shards, pad_fine, padded), F32),
            pltpu.VMEM((shards - 1, pad_fine, padded), F32),
            pltpu.VMEM((shards - 1, pad_fine, padded), F32),
            pltpu.VMEM((slabs, pad_fine, padded), F32),
            pltpu.VMEM((slabs, pad_fine, padded), F32),
            pltpu.SemaphoreType.DMA((copies,)),
            pltpu.SemaphoreType.DMA((copies,)),
        ],
        compiler_params=pltpu.CompilerParams(
            collective_id=0, has_side_effects=True, vmem_limit_bytes=40 * 1024 * 1024
        ),
    )(x, wa, wb)

    lat, coarse, dens, fine, coarse_grads = pl.pallas_call(
        store_kernel,
        out_shape=shapes,
        in_specs=[vmem] * 5,
        out_specs=(pl.BlockSpec(memory_space=pl.ANY),) * 5,
        scratch_shapes=[pltpu.SemaphoreType.DMA((5,))],
    )(*results)
    lat = jnp.transpose(lat.reshape(channels, cols // LANES, height, LANES), (0, 2, 1, 3))
    return (
        lat.reshape(1, channels, height, cols),
        coarse.reshape(1, cc, 1, width),
        dens.reshape(1),
        jnp.transpose(fine.reshape(2, 3, 3, own_fine, half), (0, 3, 4, 1, 2)),
        jnp.transpose(coarse_grads.reshape(2, 3, 3, own_coarse, mc), (0, 3, 4, 1, 2)),
    )


def solution(mesh):
    from jax.sharding import PartitionSpec as P

    in_specs = (
        P(("groups", "dp"), None, "slab", None),
        P(None, "dp", None, None, None),
        P(None, "dp", None, None, None),
    )
    out_specs = (
        P(("groups", "dp"), None, "slab", None),
        P(("groups", "dp"), None, "slab", None),
        P(("groups", "dp")),
        P("groups", "dp", None, None, None),
        P("groups", "dp", None, None, None),
    )
    return jax.shard_map(
        on_device, mesh=mesh, in_specs=in_specs, out_specs=out_specs, check_vma=False
    )
```

```python
import functools

import jax
import jax.numpy as jnp
from jax import lax
from jax.experimental import pallas as pl
from jax.experimental.pallas import tpu as pltpu

MESH = pl.DeviceIdType.MESH
F32 = jnp.float32
BF16 = jnp.bfloat16
LANES = 128


def round_up(value, step):
    return -(-value // step) * step


def product(left, right):
    return jnp.dot(left, right, preferred_element_type=F32)


def product_nt(left, right):
    return lax.dot_general(
        left, right, (((1,), (1,)), ((), ())), preferred_element_type=F32
    )


def columns_forward(rows):
    width = rows.shape[1]
    return jnp.concatenate(
        [pltpu.roll(rows, 1, 1), rows, pltpu.roll(rows, width - 1, 1)], axis=0
    )


def columns_backward(rows):
    width = rows.shape[1]
    return jnp.concatenate(
        [pltpu.roll(rows, width - 1, 1), rows, pltpu.roll(rows, 1, 1)], axis=0
    )


def split_product(value, matrix):
    count = value.shape[0]
    first = value.astype(BF16)
    rest = value - first.astype(F32)
    second = rest.astype(BF16)
    third = (rest - second.astype(F32)).astype(BF16)
    stacked = product(jnp.concatenate([first, second, third], axis=0), matrix)
    return stacked[:count] + stacked[count : 2 * count] + stacked[2 * count :]


def pool_columns(value):
    count, width = value.shape
    blocks = width // 256
    stacked = jnp.concatenate(
        [value[:, 256 * b : 256 * (b + 1)] for b in range(blocks)], axis=0
    )
    source = lax.broadcasted_iota(jnp.int32, (256, 128), 0)
    target = lax.broadcasted_iota(jnp.int32, (256, 128), 1)
    matrix = jnp.where((source >> 1) == target, 0.5, 0.0).astype(BF16)
    summed = split_product(stacked, matrix)
    return jnp.concatenate(
        [summed[count * b : count * (b + 1)] for b in range(blocks)], axis=1
    )


def unpool_columns(value):
    count, width = value.shape
    blocks = width // 128
    stacked = jnp.concatenate(
        [value[:, 128 * b : 128 * (b + 1)] for b in range(blocks)], axis=0
    )
    source = lax.broadcasted_iota(jnp.int32, (128, 256), 0)
    target = lax.broadcasted_iota(jnp.int32, (128, 256), 1)
    matrix = jnp.where((target >> 1) == source, 0.5, 0.0).astype(BF16)
    spread = split_product(stacked, matrix)
    return jnp.concatenate(
        [spread[count * b : count * (b + 1)] for b in range(blocks)], axis=1
    )


def flow_kernel(
    slabs, shards, window, own_fine, own_coarse, site_count,
    field_ref, fine_in, coarse_in,
    out_ref, coarse_ref, dens_ref, fine_ref, cgrad_ref,
    field_buf, fine_buf, coarse_buf, spaced, x_ref, c0_ref, k_buf, w_ref, cw_ref, halo0, halo1, c1_ref, tiles0, tiles1, tilesb,
    lat_ref, bend0, bend1, pool_buf, slope_ref, shalo,
    sa_ref, sb_ref, ra_buf, rb_buf, aa_buf, ab_buf,
    load_sem, send_sem, recv_sem,
):
    half = x_ref.shape[1] // 2
    mc = coarse_buf.shape[3]
    cc = 2 * mc
    patch = 9 * half
    three = 3 * half
    cpatch = 9 * mc
    tail = patch // LANES * LANES
    inset = patch - tail
    inverse = 1.0 / site_count
    me = lax.axis_index("slab")
    mine = lax.axis_index("dp")
    above = lax.rem(me + slabs - 1, slabs)
    below = lax.rem(me + 1, slabs)

    loads = [
        pltpu.make_async_copy(fine_in, fine_buf, load_sem.at[0]),
        pltpu.make_async_copy(coarse_in, coarse_buf, load_sem.at[1]),
        pltpu.make_async_copy(field_ref, field_buf, load_sem.at[2]),
    ]
    for load in loads:
        load.start()

    barrier = pltpu.get_barrier_semaphore()
    for step in range(1, slabs):
        pl.semaphore_signal(
            barrier, inc=1, device_id={"slab": lax.rem(me + step, slabs)}, device_id_type=MESH
        )
    for step in range(1, shards):
        pl.semaphore_signal(
            barrier, inc=1, device_id={"dp": lax.rem(mine + step, shards)}, device_id_type=MESH
        )
    k_buf[mine] = jnp.zeros(k_buf.shape[1:], F32)
    loads[0].wait()
    loads[1].wait()
    for l in range(2):
        for k in range(9):
            k_buf[mine, l, 0:own_fine, half * k : half * (k + 1)] = fine_buf[l, k].astype(F32)
            k_buf[mine, l, 0:own_coarse, patch + mc * k : patch + mc * (k + 1)] = coarse_buf[
                l, k
            ].astype(F32)
    loads[2].wait()
    spaced[...] = field_buf[...].astype(F32)
    tiles = x_ref.shape[2] // LANES
    for i in range(2):
        for b in range(tiles):
            x_ref[i, :, LANES * b : LANES * (b + 1)] = spaced[
                pl.ds(2 * b + i, 2 * half, stride=2 * tiles), :
            ]
        c0_ref[i] = x_ref[i, 0:half].astype(BF16)
    pl.semaphore_wait(barrier, slabs + shards - 2)

    used = [0]
    started = []

    def send(source, target, device):
        index = used[0]
        used[0] += 1
        copy = pltpu.make_async_remote_copy(
            src_ref=source,
            dst_ref=target,
            send_sem=send_sem.at[index],
            recv_sem=recv_sem.at[index],
            device_id=device,
            device_id_type=MESH,
        )
        copy.start()
        started.append(copy)
        return copy

    def to_all(gathered, axis, place, count):
        indices = []
        for step in range(1, count):
            indices.append(used[0])
            send(gathered.at[place], gathered.at[place], {axis: lax.rem(place + step, count)})
        return indices

    def from_all(gathered, axis, place, count, indices):
        for step in range(1, count):
            source = lax.rem(place - step + count, count)
            pltpu.make_async_remote_copy(
                src_ref=gathered.at[place],
                dst_ref=gathered.at[source],
                send_sem=send_sem.at[indices[step - 1]],
                recv_sem=recv_sem.at[indices[step - 1]],
                device_id={axis: source},
                device_id_type=MESH,
            ).wait_recv()

    k_copies = to_all(k_buf, "dp", mine, shards)
    from_above = send(c0_ref.at[1], halo0.at[0], {"slab": below})
    from_below = send(c0_ref.at[0], halo0.at[1], {"slab": above})

    sa_ref[...] = jnp.zeros_like(sa_ref)
    sb_ref[...] = jnp.zeros_like(sb_ref)

    def set_tile(tiles, index, rows, turn):
        tiles[three * index : three * (index + 1), :] = turn(rows).astype(BF16)

    def turned_over(value, count, start):
        filler = jnp.zeros((LANES - value.shape[0], value.shape[1]), F32)
        flipped = jnp.transpose(jnp.concatenate([value, filler], axis=0))
        parts = [
            flipped[start + count * k : start + count * (k + 1), 0:count] for k in range(9)
        ]
        return jnp.concatenate(parts, axis=1)

    def own_terms(weight, tiles, first, second):
        stacked = jnp.concatenate(
            [weight[:, first : first + 2 * three], weight[:, second : second + 2 * three]], axis=0
        ).astype(BF16)
        both = product(stacked, tiles[three : 3 * three, :])
        return both[0:half], both[half:]

    for i in range(2):
        set_tile(tiles0, i + 1, x_ref[i, 0:half].astype(F32), columns_forward)
    from_all(k_buf, "dp", mine, shards, k_copies)
    for d in range(shards):
        for l in range(2):
            w_ref[l, own_fine * d : own_fine * (d + 1)] = k_buf[d, l, 0:own_fine]
            cw_ref[l, own_coarse * d : own_coarse * (d + 1)] = k_buf[d, l, 0:own_coarse, tail:]
    total = w_ref[0]
    sums = own_terms(total, tiles0, three, 0)
    edges = [total[:, 0:three].astype(BF16), total[:, 2 * three : patch].astype(BF16)]
    from_above.wait_recv()
    set_tile(tiles0, 0, halo0[0].astype(F32), columns_forward)
    from_below.wait_recv()
    set_tile(tiles0, 3, halo0[1].astype(F32), columns_forward)
    density = jnp.zeros((half, x_ref.shape[2]), F32)
    for i in range(2):
        edge = three * 3 * i
        bent = jnp.tanh(sums[i] + product(edges[i], tiles0[edge : edge + three, :]))
        moved = x_ref[i, half:].astype(F32) + bent
        c1_ref[i] = moved.astype(BF16)
        lat_ref[i, half:] = moved
        bend0[i] = 1.0 - bent * bent
    from_above = send(c1_ref.at[1], halo1.at[0], {"slab": below})
    from_below = send(c1_ref.at[0], halo1.at[1], {"slab": above})

    for i in range(2):
        set_tile(tiles1, i + 1, c1_ref[i].astype(F32), columns_forward)
        moved = lat_ref[i, half:]
        density = density + moved * moved
    weight1 = w_ref[1]
    sums = own_terms(weight1, tiles1, three, 0)
    edges = [weight1[:, 0:three].astype(BF16), weight1[:, 2 * three : patch].astype(BF16)]
    coarse_weights = total[2 * half :, 0:cpatch]
    cfor0, cfor1, cback1, cback0 = [
        coarse_weights[mc * k : mc * (k + 1)].astype(BF16) for k in range(4)
    ]
    back1 = turned_over(w_ref[1], half, 0)
    cback0, cback1 = [turned_over(cw_ref[l], mc, inset).astype(BF16) for l in range(2)]
    from_above.wait_recv()
    set_tile(tiles1, 0, halo1[0].astype(F32), columns_forward)
    from_below.wait_recv()
    set_tile(tiles1, 3, halo1[1].astype(F32), columns_forward)
    sums = [
        sums[i] + product(edges[i], tiles1[three * 3 * i : three * (3 * i + 1), :])
        for i in range(2)
    ]

    def finish(part):
        for i in range(2):
            bent = jnp.tanh(sums[i][part])
            lat_ref[i, part] = x_ref[i, part].astype(F32) + bent
            bend1[i, part] = 1.0 - bent * bent

    finish(slice(0, cc))

    pool_buf[0] = pool_columns(lat_ref[0, 0:cc] + lat_ref[1, 0:cc])
    pool_copies = []
    for k in range(1, window):
        offset = k if k <= window // 2 else k - window
        peer = lax.rem(me - offset + slabs, slabs)
        pool_copies.append(send(pool_buf.at[0], pool_buf.at[k], {"slab": peer}))
    finish(slice(cc, half))
    for i in range(2):
        slope_ref[i, cc:half] = (lat_ref[i, cc:half] * inverse * bend1[i, cc:half]).astype(BF16)
    high_above = send(slope_ref.at[1, cc:half], shalo.at[0, cc:half], {"slab": below})
    high_below = send(slope_ref.at[0, cc:half], shalo.at[1, cc:half], {"slab": above})
    for i in range(2):
        moved = lat_ref[i, 0:half]
        density = density + moved * moved
        for b in range(tiles):
            out_ref[pl.ds(2 * b + i, 2 * half, stride=2 * tiles), :] = lat_ref[
                i, :, LANES * b : LANES * (b + 1)
            ]
    for copy in pool_copies:
        copy.wait_recv()

    cfor0, cfor1 = [cw_ref[l, :, inset : inset + cpatch].astype(BF16) for l in range(2)]

    width = pool_buf.shape[2]

    def coarse_patches(rows, turn, sign, wanted):
        turned = [turn(row) for row in rows]
        columns = []
        for k in wanted:
            near = [turned[(k + sign * (p - 1)) % window] for p in range(3)]
            columns.append(jnp.concatenate(near, axis=0))
        return jnp.concatenate(columns, axis=1)

    def cut(value):
        return [value[:, width * k : width * (k + 1)] for k in range(value.shape[1] // width)]

    def rounded(value):
        return value.astype(BF16).astype(F32)

    everything = range(window)
    low = jnp.concatenate([pool_buf[k, 0:mc] for k in everything], axis=1)
    high = jnp.concatenate([pool_buf[k, mc:cc] for k in everything], axis=1)
    patches0 = coarse_patches(cut(rounded(low)), columns_forward, 1, everything)
    bent_c0 = jnp.tanh(product(cfor0, patches0.astype(BF16)))
    high = high + bent_c0
    patches1 = coarse_patches(cut(rounded(high)), columns_forward, 1, everything)
    bent_c1 = jnp.tanh(product(cfor1, patches1.astype(BF16)))
    low = low + bent_c1
    coarse_own = jnp.concatenate([low[:, 0:width], high[:, 0:width]], axis=0)
    for b in range(width // LANES):
        coarse_ref[pl.ds(b, cc, stride=width // LANES), :] = coarse_own[
            :, LANES * b : LANES * (b + 1)
        ]
    pooled = pool_buf[0]

    def coarse_kernel_grad(slope, patches):
        widened = jnp.concatenate(
            [
                jnp.zeros((inset, width), F32),
                patches[:, 0:width],
                jnp.zeros((LANES - inset - cpatch, width), F32),
            ],
            axis=0,
        )
        return product_nt(slope[:, 0:width], widened.astype(BF16))

    grad_low = low * inverse
    slope_c1 = (grad_low * (1.0 - bent_c1 * bent_c1)).astype(BF16)
    kernel_c1 = coarse_kernel_grad(slope_c1, patches1)
    back_patches = coarse_patches(cut(slope_c1.astype(F32)), columns_backward, -1, everything)
    grad_high = high * inverse + product(cback1, back_patches.astype(BF16))
    slope_c0 = (grad_high * (1.0 - bent_c0 * bent_c0)).astype(BF16)
    kernel_c0 = coarse_kernel_grad(slope_c0, patches0)
    back_patches = coarse_patches(cut(slope_c0.astype(F32)), columns_backward, -1, [0])
    grad_own = grad_low[:, 0:width] + product(cback0, back_patches.astype(BF16))
    pooled_grad = jnp.concatenate([grad_own, grad_high[:, 0:width]], axis=0) - pooled * inverse
    spread = unpool_columns(pooled_grad)

    for i in range(2):
        slope_ref[i, 0:cc] = ((lat_ref[i, 0:cc] * inverse + spread) * bend1[i, 0:cc]).astype(BF16)
    low_above = send(slope_ref.at[1, 0:cc], shalo.at[0, 0:cc], {"slab": below})
    low_below = send(slope_ref.at[0, 0:cc], shalo.at[1, 0:cc], {"slab": above})
    kernel_1 = product_nt(slope_ref[0], tiles1[0:patch, :])
    kernel_1 = kernel_1 + product_nt(slope_ref[1], tiles1[three : three + patch, :])
    for d in range(shards):
        sb_ref[d, 0:own_fine, 0:patch] = kernel_1[own_fine * d : own_fine * (d + 1)]
        for l, kernel_c in enumerate((kernel_c0, kernel_c1)):
            place = slice(own_coarse * l, own_coarse * (l + 1))
            sb_ref[d, place, tail:] = (
                sb_ref[d, place, tail:] + kernel_c[own_coarse * d : own_coarse * (d + 1)]
            )
    rb_copies = []
    for step in range(1, shards):
        peer = lax.rem(mine + step, shards)
        rb_copies.append(send(sb_ref.at[peer], rb_buf.at[step - 1], {"dp": peer}))
    for i in range(2):
        set_tile(tilesb, 2 - i, slope_ref[i].astype(F32), columns_backward)

    folded = density[0:8]
    for b in range(1, half // 8):
        folded = folded + density[8 * b : 8 * (b + 1)]
    narrow = folded[:, 0:width] + folded[:, width:]
    for b in range(cc // 8):
        part = slice(8 * b, 8 * (b + 1))
        narrow = narrow - pooled[part] * pooled[part] + coarse_own[part] * coarse_own[part]
    tile = narrow[:, 0:LANES]
    for b in range(1, width // LANES):
        tile = tile + narrow[:, LANES * b : LANES * (b + 1)]
    site_density = jnp.sum(tile * (0.5 * inverse), keepdims=True)
    sums = own_terms(back1, tilesb, 0, three)
    edges = [back1[:, 2 * three : patch].astype(BF16), back1[:, 0:three].astype(BF16)]

    high_above.wait_recv()
    low_above.wait_recv()
    set_tile(tilesb, 3, shalo[0].astype(F32), columns_backward)
    high_below.wait_recv()
    low_below.wait_recv()
    set_tile(tilesb, 0, shalo[1].astype(F32), columns_backward)
    kernel_0 = None
    for i in range(2):
        edge = three * 3 * (1 - i)
        grad = (
            lat_ref[i, half:] * inverse
            + sums[i]
            + product(edges[i], tilesb[edge : edge + three, :])
        )
        slope = (grad * bend0[i]).astype(BF16)
        term = product_nt(slope, tiles0[three * i : three * i + patch, :])
        kernel_0 = term if kernel_0 is None else kernel_0 + term
    for d in range(shards):
        sa_ref[d, 0:own_fine, 0:patch] = kernel_0[own_fine * d : own_fine * (d + 1)]
    ra_copies = []
    for step in range(1, shards):
        peer = lax.rem(mine + step, shards)
        ra_copies.append(send(sa_ref.at[peer], ra_buf.at[step - 1], {"dp": peer}))

    block = sb_ref[mine]
    for step in range(1, shards):
        rb_copies[step - 1].wait_recv()
        block = block + rb_buf[step - 1]
    row = lax.broadcasted_iota(jnp.int32, block.shape, 0)
    lane = lax.broadcasted_iota(jnp.int32, block.shape, 1)
    ab_buf[me] = jnp.where((row == 2 * own_coarse) & (lane == patch), site_density, block)
    ab_copies = to_all(ab_buf, "slab", me, slabs)
    block = sa_ref[mine]
    for step in range(1, shards):
        ra_copies[step - 1].wait_recv()
        block = block + ra_buf[step - 1]
    aa_buf[me] = block
    aa_copies = to_all(aa_buf, "slab", me, slabs)

    from_all(ab_buf, "slab", me, slabs, ab_copies)
    block = ab_buf[0]
    for s in range(1, slabs):
        block = block + ab_buf[s]
    dens_ref[...] = block[2 * own_coarse : 2 * own_coarse + 1, patch : patch + 1]
    for k in range(9):
        fine_ref[1, k] = block[0:own_fine, half * k : half * (k + 1)]
        for l in range(2):
            cgrad_ref[l, k] = block[
                own_coarse * l : own_coarse * (l + 1), patch + mc * k : patch + mc * (k + 1)
            ]
    from_all(aa_buf, "slab", me, slabs, aa_copies)
    block = aa_buf[0]
    for s in range(1, slabs):
        block = block + aa_buf[s]
    for k in range(9):
        fine_ref[0, k] = block[0:own_fine, half * k : half * (k + 1)]
    for copy in started:
        copy.wait_send()


def store_kernel(*refs):
    sem = refs[-1]
    copies = [pltpu.make_async_copy(refs[k], refs[5 + k], sem.at[k]) for k in range(5)]
    for copy in copies:
        copy.start()
    for copy in copies:
        copy.wait()


def on_device(lattice_field, fine_kernels, coarse_kernels):
    slabs, shards = lax.axis_size("slab"), lax.axis_size("dp")
    _, channels, height, cols = lattice_field.shape
    _, own_fine, half, _, _ = fine_kernels.shape
    _, own_coarse, mc, _, _ = coarse_kernels.shape
    cc, width = 2 * mc, cols // 2
    patch, cpatch = 9 * half, 9 * mc
    padded = round_up(patch, LANES)
    site_count = height * slabs * cols
    window = min(slabs, 9)

    field = lattice_field.reshape(channels, height, cols // LANES, LANES)
    field = jnp.transpose(field, (0, 2, 1, 3)).reshape(-1, LANES)
    fine_in = jnp.transpose(fine_kernels, (0, 3, 4, 1, 2)).reshape(2, 9, own_fine, half)
    coarse_in = jnp.transpose(coarse_kernels, (0, 3, 4, 1, 2)).reshape(2, 9, own_coarse, mc)

    pad_fine = round_up(own_fine, 8)
    tall = channels * height * cols // LANES
    copies = 3 * (shards - 1) + 8 + (window - 1) + 2 * (slabs - 1)
    vmem = pl.BlockSpec(memory_space=pltpu.VMEM)
    shapes = (
        jax.ShapeDtypeStruct((tall, LANES), F32),
        jax.ShapeDtypeStruct((cc * width // LANES, LANES), F32),
        jax.ShapeDtypeStruct((1, 1), F32),
        jax.ShapeDtypeStruct((2, 9, own_fine, half), F32),
        jax.ShapeDtypeStruct((2, 9, own_coarse, mc), F32),
    )
    results = pl.pallas_call(
        functools.partial(
            flow_kernel, slabs, shards, window, own_fine, own_coarse, site_count
        ),
        out_shape=shapes,
        in_specs=[pl.BlockSpec(memory_space=pltpu.HBM)] * 3,
        out_specs=(vmem,) * 5,
        scratch_shapes=[
            pltpu.VMEM(field.shape, BF16),
            pltpu.VMEM(fine_in.shape, BF16),
            pltpu.VMEM(coarse_in.shape, BF16),
            pltpu.VMEM(field.shape, F32),
            pltpu.VMEM((2, channels, cols), F32),
            pltpu.VMEM((2, half, cols), BF16),
            pltpu.VMEM((shards, 2, pad_fine, padded), F32),
            pltpu.VMEM((2, half, padded), F32),
            pltpu.VMEM((2, mc, LANES), F32),
            pltpu.VMEM((2, half, cols), BF16),
            pltpu.VMEM((2, half, cols), BF16),
            pltpu.VMEM((2, half, cols), BF16),
            pltpu.VMEM((12 * half, cols), BF16),
            pltpu.VMEM((12 * half, cols), BF16),
            pltpu.VMEM((12 * half, cols), BF16),
            pltpu.VMEM((2, channels, cols), F32),
            pltpu.VMEM((2, half, cols), F32),
            pltpu.VMEM((2, half, cols), F32),
            pltpu.VMEM((window, cc, width), F32),
            pltpu.VMEM((2, half, cols), BF16),
            pltpu.VMEM((2, half, cols), BF16),
            pltpu.VMEM((shards, pad_fine, padded), F32),
            pltpu.VMEM((shards, pad_fine, padded), F32),
            pltpu.VMEM((shards - 1, pad_fine, padded), F32),
            pltpu.VMEM((shards - 1, pad_fine, padded), F32),
            pltpu.VMEM((slabs, pad_fine, padded), F32),
            pltpu.VMEM((slabs, pad_fine, padded), F32),
            pltpu.SemaphoreType.DMA((3,)),
            pltpu.SemaphoreType.DMA((copies,)),
            pltpu.SemaphoreType.DMA((copies,)),
        ],
        compiler_params=pltpu.CompilerParams(
            collective_id=0, has_side_effects=True, vmem_limit_bytes=40 * 1024 * 1024
        ),
    )(field, fine_in, coarse_in)
    lat, coarse, dens, fine, coarse_grads = pl.pallas_call(
        store_kernel,
        out_shape=shapes,
        in_specs=[pl.BlockSpec(memory_space=pl.ANY)] * 5,
        out_specs=(pl.BlockSpec(memory_space=pltpu.HBM),) * 5,
        scratch_shapes=[pltpu.SemaphoreType.DMA((5,))],
        compiler_params=pltpu.CompilerParams(vmem_limit_bytes=1024 * 1024),
    )(*results)

    lat = jnp.transpose(lat.reshape(channels, cols // LANES, height, LANES), (0, 2, 1, 3))
    return (
        lat.reshape(1, channels, height, cols),
        coarse.reshape(1, cc, 1, width),
        dens.reshape(1),
        jnp.transpose(fine.reshape(2, 3, 3, own_fine, half), (0, 3, 4, 1, 2)),
        jnp.transpose(coarse_grads.reshape(2, 3, 3, own_coarse, mc), (0, 3, 4, 1, 2)),
    )


def solution(mesh):
    from jax.sharding import PartitionSpec as P

    in_specs = (
        P(("groups", "dp"), None, "slab", None),
        P(None, "dp", None, None, None),
        P(None, "dp", None, None, None),
    )
    out_specs = (
        P(("groups", "dp"), None, "slab", None),
        P(("groups", "dp"), None, "slab", None),
        P(("groups", "dp")),
        P("groups", "dp", None, None, None),
        P("groups", "dp", None, None, None),
    )
    return jax.shard_map(
        on_device, mesh=mesh, in_specs=in_specs, out_specs=out_specs, check_vma=False
    )
```

```python
import functools

import jax
import jax.numpy as jnp
from jax import lax
from jax.experimental import pallas as pl
from jax.experimental.pallas import tpu as pltpu

MESH = pl.DeviceIdType.MESH
F32 = jnp.float32
BF16 = jnp.bfloat16
LANES = 128


def round_up(value, step):
    return -(-value // step) * step


def product(left, right):
    return jnp.dot(left, right, preferred_element_type=F32)


def product_nt(left, right):
    return lax.dot_general(
        left, right, (((1,), (1,)), ((), ())), preferred_element_type=F32
    )


def columns_forward(rows):
    width = rows.shape[1]
    return jnp.concatenate(
        [pltpu.roll(rows, 1, 1), rows, pltpu.roll(rows, width - 1, 1)], axis=0
    )


def columns_backward(rows):
    width = rows.shape[1]
    return jnp.concatenate(
        [pltpu.roll(rows, width - 1, 1), rows, pltpu.roll(rows, 1, 1)], axis=0
    )


def split_product(value, matrix):
    count = value.shape[0]
    first = value.astype(BF16)
    rest = value - first.astype(F32)
    second = rest.astype(BF16)
    third = (rest - second.astype(F32)).astype(BF16)
    stacked = product(jnp.concatenate([first, second, third], axis=0), matrix)
    return stacked[:count] + stacked[count : 2 * count] + stacked[2 * count :]


def pool_columns(value):
    count, width = value.shape
    blocks = width // 256
    stacked = jnp.concatenate(
        [value[:, 256 * b : 256 * (b + 1)] for b in range(blocks)], axis=0
    )
    source = lax.broadcasted_iota(jnp.int32, (256, 128), 0)
    target = lax.broadcasted_iota(jnp.int32, (256, 128), 1)
    matrix = jnp.where((source >> 1) == target, 0.5, 0.0).astype(BF16)
    summed = split_product(stacked, matrix)
    return jnp.concatenate(
        [summed[count * b : count * (b + 1)] for b in range(blocks)], axis=1
    )


def unpool_columns(value):
    count, width = value.shape
    blocks = width // 128
    stacked = jnp.concatenate(
        [value[:, 128 * b : 128 * (b + 1)] for b in range(blocks)], axis=0
    )
    source = lax.broadcasted_iota(jnp.int32, (128, 256), 0)
    target = lax.broadcasted_iota(jnp.int32, (128, 256), 1)
    matrix = jnp.where((target >> 1) == source, 0.5, 0.0).astype(BF16)
    spread = split_product(stacked, matrix)
    return jnp.concatenate(
        [spread[count * b : count * (b + 1)] for b in range(blocks)], axis=1
    )


def flow_kernel(
    slabs, shards, window, own_fine, own_coarse, site_count,
    field_ref, fine_in, coarse_in,
    out_ref, coarse_ref, dens_ref, fine_ref, cgrad_ref,
    field_buf, fine_buf, coarse_buf, spaced, x_ref, c0_ref, k_buf, w_ref, cw_ref, halo0, halo1, c1_ref, tiles0, tiles1, tilesb,
    lat_ref, bend0, bend1, pool_buf, slope_ref, base_ref, shalo,
    sa_ref, sb_ref, ra_buf, rb_buf, aa_buf, ab_buf,
    load_sem, send_sem, recv_sem,
):
    half = x_ref.shape[1] // 2
    mc = coarse_buf.shape[3]
    cc = 2 * mc
    patch = 9 * half
    three = 3 * half
    cpatch = 9 * mc
    tail = patch // LANES * LANES
    inset = patch - tail
    inverse = 1.0 / site_count
    me = lax.axis_index("slab")
    mine = lax.axis_index("dp")
    above = lax.rem(me + slabs - 1, slabs)
    below = lax.rem(me + 1, slabs)

    loads = [
        pltpu.make_async_copy(fine_in, fine_buf, load_sem.at[0]),
        pltpu.make_async_copy(coarse_in, coarse_buf, load_sem.at[1]),
        pltpu.make_async_copy(field_ref, field_buf, load_sem.at[2]),
    ]
    for load in loads:
        load.start()

    barrier = pltpu.get_barrier_semaphore()
    for step in range(1, slabs):
        pl.semaphore_signal(
            barrier, inc=1, device_id={"slab": lax.rem(me + step, slabs)}, device_id_type=MESH
        )
    for step in range(1, shards):
        pl.semaphore_signal(
            barrier, inc=1, device_id={"dp": lax.rem(mine + step, shards)}, device_id_type=MESH
        )
    k_buf[mine] = jnp.zeros(k_buf.shape[1:], F32)
    loads[0].wait()
    loads[1].wait()
    for l in range(2):
        for k in range(9):
            k_buf[mine, l, 0:own_fine, half * k : half * (k + 1)] = fine_buf[l, k].astype(F32)
            k_buf[mine, l, 0:own_coarse, patch + mc * k : patch + mc * (k + 1)] = coarse_buf[
                l, k
            ].astype(F32)
    loads[2].wait()
    spaced[...] = field_buf[...].astype(F32)
    tiles = x_ref.shape[2] // LANES
    for i in range(2):
        for b in range(tiles):
            x_ref[i, :, LANES * b : LANES * (b + 1)] = spaced[
                pl.ds(2 * b + i, 2 * half, stride=2 * tiles), :
            ]
        c0_ref[i] = x_ref[i, 0:half].astype(BF16)
    pl.semaphore_wait(barrier, slabs + shards - 2)

    used = [0]
    started = []

    def send(source, target, device):
        index = used[0]
        used[0] += 1
        copy = pltpu.make_async_remote_copy(
            src_ref=source,
            dst_ref=target,
            send_sem=send_sem.at[index],
            recv_sem=recv_sem.at[index],
            device_id=device,
            device_id_type=MESH,
        )
        copy.start()
        started.append(copy)
        return copy

    def to_all(gathered, axis, place, count):
        indices = []
        for step in range(1, count):
            indices.append(used[0])
            send(gathered.at[place], gathered.at[place], {axis: lax.rem(place + step, count)})
        return indices

    def from_all(gathered, axis, place, count, indices):
        for step in range(1, count):
            source = lax.rem(place - step + count, count)
            pltpu.make_async_remote_copy(
                src_ref=gathered.at[place],
                dst_ref=gathered.at[source],
                send_sem=send_sem.at[indices[step - 1]],
                recv_sem=recv_sem.at[indices[step - 1]],
                device_id={axis: source},
                device_id_type=MESH,
            ).wait_recv()

    k_copies = to_all(k_buf, "dp", mine, shards)
    from_above = send(c0_ref.at[1], halo0.at[0], {"slab": below})
    from_below = send(c0_ref.at[0], halo0.at[1], {"slab": above})

    sa_ref[...] = jnp.zeros_like(sa_ref)
    sb_ref[...] = jnp.zeros_like(sb_ref)

    def set_tile(tiles, index, rows, turn):
        tiles[three * index : three * (index + 1), :] = turn(rows).astype(BF16)

    def turned_over(value, count, start):
        filler = jnp.zeros((LANES - value.shape[0], value.shape[1]), F32)
        flipped = jnp.transpose(jnp.concatenate([value, filler], axis=0))
        parts = [
            flipped[start + count * k : start + count * (k + 1), 0:count] for k in range(9)
        ]
        return jnp.concatenate(parts, axis=1)

    def own_terms(weight, tiles, first, second):
        stacked = jnp.concatenate(
            [weight[:, first : first + 2 * three], weight[:, second : second + 2 * three]], axis=0
        ).astype(BF16)
        both = product(stacked, tiles[three : 3 * three, :])
        return both[0:half], both[half:]

    for i in range(2):
        set_tile(tiles0, i + 1, x_ref[i, 0:half].astype(F32), columns_forward)
    from_all(k_buf, "dp", mine, shards, k_copies)
    for d in range(shards):
        for l in range(2):
            w_ref[l, own_fine * d : own_fine * (d + 1)] = k_buf[d, l, 0:own_fine]
            cw_ref[l, own_coarse * d : own_coarse * (d + 1)] = k_buf[d, l, 0:own_coarse, tail:]
    total = w_ref[0]
    sums = own_terms(total, tiles0, three, 0)
    edges = [total[:, 0:three].astype(BF16), total[:, 2 * three : patch].astype(BF16)]
    from_above.wait_recv()
    set_tile(tiles0, 0, halo0[0].astype(F32), columns_forward)
    from_below.wait_recv()
    set_tile(tiles0, 3, halo0[1].astype(F32), columns_forward)
    density = jnp.zeros((half, x_ref.shape[2]), F32)
    for i in range(2):
        edge = three * 3 * i
        bent = jnp.tanh(sums[i] + product(edges[i], tiles0[edge : edge + three, :]))
        moved = x_ref[i, half:].astype(F32) + bent
        c1_ref[i] = moved.astype(BF16)
        lat_ref[i, half:] = moved
        bend0[i] = 1.0 - bent * bent
    from_above = send(c1_ref.at[1], halo1.at[0], {"slab": below})
    from_below = send(c1_ref.at[0], halo1.at[1], {"slab": above})

    for i in range(2):
        set_tile(tiles1, i + 1, c1_ref[i].astype(F32), columns_forward)
        moved = lat_ref[i, half:]
        density = density + moved * moved
    weight1 = w_ref[1]
    sums = own_terms(weight1, tiles1, three, 0)
    edges = [weight1[:, 0:three].astype(BF16), weight1[:, 2 * three : patch].astype(BF16)]
    coarse_weights = total[2 * half :, 0:cpatch]
    cfor0, cfor1, cback1, cback0 = [
        coarse_weights[mc * k : mc * (k + 1)].astype(BF16) for k in range(4)
    ]
    back1 = turned_over(w_ref[1], half, 0)
    cback0, cback1 = [turned_over(cw_ref[l], mc, inset).astype(BF16) for l in range(2)]
    from_above.wait_recv()
    set_tile(tiles1, 0, halo1[0].astype(F32), columns_forward)
    from_below.wait_recv()
    set_tile(tiles1, 3, halo1[1].astype(F32), columns_forward)
    sums = [
        sums[i] + product(edges[i], tiles1[three * 3 * i : three * (3 * i + 1), :])
        for i in range(2)
    ]

    def finish(part):
        for i in range(2):
            bent = jnp.tanh(sums[i][part])
            lat_ref[i, part] = x_ref[i, part].astype(F32) + bent
            bend1[i, part] = 1.0 - bent * bent

    finish(slice(0, cc))

    pool_buf[0] = pool_columns(lat_ref[0, 0:cc] + lat_ref[1, 0:cc])
    pool_copies = []
    for k in range(1, window):
        offset = k if k <= window // 2 else k - window
        peer = lax.rem(me - offset + slabs, slabs)
        pool_copies.append(send(pool_buf.at[0], pool_buf.at[k], {"slab": peer}))
    finish(slice(cc, half))
    for i in range(2):
        base = (lat_ref[i, 0:half] * inverse * bend1[i]).astype(BF16)
        base_ref[i, 0:half] = base
        base_ref[i, half:] = bend1[i, 0:cc].astype(BF16)
        slope_ref[i, cc:half] = base[cc:half]
    from_above = send(base_ref.at[1], shalo.at[0], {"slab": below})
    from_below = send(base_ref.at[0], shalo.at[1], {"slab": above})
    for i in range(2):
        moved = lat_ref[i, 0:half]
        density = density + moved * moved
        for b in range(tiles):
            out_ref[pl.ds(2 * b + i, 2 * half, stride=2 * tiles), :] = lat_ref[
                i, :, LANES * b : LANES * (b + 1)
            ]
    for copy in pool_copies:
        copy.wait_recv()

    cfor0, cfor1 = [cw_ref[l, :, inset : inset + cpatch].astype(BF16) for l in range(2)]

    width = pool_buf.shape[2]

    def coarse_patches(rows, turn, sign, wanted):
        turned = [turn(row) for row in rows]
        columns = []
        for k in wanted:
            near = [turned[(k + sign * (p - 1)) % window] for p in range(3)]
            columns.append(jnp.concatenate(near, axis=0))
        return jnp.concatenate(columns, axis=1)

    def cut(value):
        return [value[:, width * k : width * (k + 1)] for k in range(value.shape[1] // width)]

    def rounded(value):
        return value.astype(BF16).astype(F32)

    everything = range(window)
    low = jnp.concatenate([pool_buf[k, 0:mc] for k in everything], axis=1)
    high = jnp.concatenate([pool_buf[k, mc:cc] for k in everything], axis=1)
    patches0 = coarse_patches(cut(rounded(low)), columns_forward, 1, everything)
    bent_c0 = jnp.tanh(product(cfor0, patches0.astype(BF16)))
    high = high + bent_c0
    patches1 = coarse_patches(cut(rounded(high)), columns_forward, 1, everything)
    bent_c1 = jnp.tanh(product(cfor1, patches1.astype(BF16)))
    low = low + bent_c1
    coarse_own = jnp.concatenate([low[:, 0:width], high[:, 0:width]], axis=0)
    for b in range(width // LANES):
        coarse_ref[pl.ds(b, cc, stride=width // LANES), :] = coarse_own[
            :, LANES * b : LANES * (b + 1)
        ]
    pooled = pool_buf[0]

    def coarse_kernel_grad(slope, patches):
        widened = jnp.concatenate(
            [
                jnp.zeros((inset, width), F32),
                patches[:, 0:width],
                jnp.zeros((LANES - inset - cpatch, width), F32),
            ],
            axis=0,
        )
        return product_nt(slope[:, 0:width], widened.astype(BF16))

    grad_low = low * inverse
    slope_c1 = (grad_low * (1.0 - bent_c1 * bent_c1)).astype(BF16)
    kernel_c1 = coarse_kernel_grad(slope_c1, patches1)
    back_patches = coarse_patches(cut(slope_c1.astype(F32)), columns_backward, -1, everything)
    grad_high = high * inverse + product(cback1, back_patches.astype(BF16))
    slope_c0 = (grad_high * (1.0 - bent_c0 * bent_c0)).astype(BF16)
    kernel_c0 = coarse_kernel_grad(slope_c0, patches0)
    wanted = [0, 1, window - 1]
    back_patches = coarse_patches(cut(slope_c0.astype(F32)), columns_backward, -1, wanted)

    def chosen(value):
        pieces = cut(value)
        return jnp.concatenate([pieces[k] for k in wanted], axis=1)

    pooled_three = jnp.concatenate([pool_buf[k] for k in wanted], axis=1)
    grad_three = chosen(grad_low) + product(cback0, back_patches.astype(BF16))
    grad_three = jnp.concatenate([grad_three, chosen(grad_high)], axis=0)
    spread_three = unpool_columns(grad_three - pooled_three * inverse)
    cols = x_ref.shape[2]
    spread, spread_below, spread_above = [
        spread_three[:, cols * k : cols * (k + 1)] for k in range(3)
    ]

    for i in range(2):
        slope_ref[i, 0:cc] = ((lat_ref[i, 0:cc] * inverse + spread) * bend1[i, 0:cc]).astype(BF16)
    kernel_1 = product_nt(slope_ref[0], tiles1[0:patch, :])
    kernel_1 = kernel_1 + product_nt(slope_ref[1], tiles1[three : three + patch, :])
    for d in range(shards):
        sb_ref[d, 0:own_fine, 0:patch] = kernel_1[own_fine * d : own_fine * (d + 1)]
        for l, kernel_c in enumerate((kernel_c0, kernel_c1)):
            place = slice(own_coarse * l, own_coarse * (l + 1))
            sb_ref[d, place, tail:] = (
                sb_ref[d, place, tail:] + kernel_c[own_coarse * d : own_coarse * (d + 1)]
            )
    rb_copies = []
    for step in range(1, shards):
        peer = lax.rem(mine + step, shards)
        rb_copies.append(send(sb_ref.at[peer], rb_buf.at[step - 1], {"dp": peer}))
    for i in range(2):
        set_tile(tilesb, 2 - i, slope_ref[i].astype(F32), columns_backward)

    folded = density[0:8]
    for b in range(1, half // 8):
        folded = folded + density[8 * b : 8 * (b + 1)]
    narrow = folded[:, 0:width] + folded[:, width:]
    for b in range(cc // 8):
        part = slice(8 * b, 8 * (b + 1))
        narrow = narrow - pooled[part] * pooled[part] + coarse_own[part] * coarse_own[part]
    tile = narrow[:, 0:LANES]
    for b in range(1, width // LANES):
        tile = tile + narrow[:, LANES * b : LANES * (b + 1)]
    site_density = jnp.sum(tile * (0.5 * inverse), keepdims=True)
    sums = own_terms(back1, tilesb, 0, three)
    edges = [back1[:, 2 * three : patch].astype(BF16), back1[:, 0:three].astype(BF16)]

    def edge_slope(index, addition):
        low = shalo[index, 0:cc].astype(F32) + addition * shalo[index, half:].astype(F32)
        return jnp.concatenate([rounded(low), shalo[index, cc:half].astype(F32)], axis=0)

    from_above.wait_recv()
    set_tile(tilesb, 3, edge_slope(0, spread_above), columns_backward)
    from_below.wait_recv()
    set_tile(tilesb, 0, edge_slope(1, spread_below), columns_backward)
    kernel_0 = None
    for i in range(2):
        edge = three * 3 * (1 - i)
        grad = (
            lat_ref[i, half:] * inverse
            + sums[i]
            + product(edges[i], tilesb[edge : edge + three, :])
        )
        slope = (grad * bend0[i]).astype(BF16)
        term = product_nt(slope, tiles0[three * i : three * i + patch, :])
        kernel_0 = term if kernel_0 is None else kernel_0 + term
    for d in range(shards):
        sa_ref[d, 0:own_fine, 0:patch] = kernel_0[own_fine * d : own_fine * (d + 1)]
    ra_copies = []
    for step in range(1, shards):
        peer = lax.rem(mine + step, shards)
        ra_copies.append(send(sa_ref.at[peer], ra_buf.at[step - 1], {"dp": peer}))

    block = sb_ref[mine]
    for step in range(1, shards):
        rb_copies[step - 1].wait_recv()
        block = block + rb_buf[step - 1]
    row = lax.broadcasted_iota(jnp.int32, block.shape, 0)
    lane = lax.broadcasted_iota(jnp.int32, block.shape, 1)
    ab_buf[me] = jnp.where((row == 2 * own_coarse) & (lane == patch), site_density, block)
    ab_copies = to_all(ab_buf, "slab", me, slabs)
    block = sa_ref[mine]
    for step in range(1, shards):
        ra_copies[step - 1].wait_recv()
        block = block + ra_buf[step - 1]
    aa_buf[me] = block
    aa_copies = to_all(aa_buf, "slab", me, slabs)

    from_all(ab_buf, "slab", me, slabs, ab_copies)
    block = ab_buf[0]
    for s in range(1, slabs):
        block = block + ab_buf[s]
    dens_ref[...] = block[2 * own_coarse : 2 * own_coarse + 1, patch : patch + 1]
    for k in range(9):
        fine_ref[1, k] = block[0:own_fine, half * k : half * (k + 1)]
        for l in range(2):
            cgrad_ref[l, k] = block[
                own_coarse * l : own_coarse * (l + 1), patch + mc * k : patch + mc * (k + 1)
            ]
    from_all(aa_buf, "slab", me, slabs, aa_copies)
    block = aa_buf[0]
    for s in range(1, slabs):
        block = block + aa_buf[s]
    for k in range(9):
        fine_ref[0, k] = block[0:own_fine, half * k : half * (k + 1)]
    for copy in started:
        copy.wait_send()


def store_kernel(*refs):
    sem = refs[-1]
    copies = [pltpu.make_async_copy(refs[k], refs[5 + k], sem.at[k]) for k in range(5)]
    for copy in copies:
        copy.start()
    for copy in copies:
        copy.wait()


def on_device(lattice_field, fine_kernels, coarse_kernels):
    slabs, shards = lax.axis_size("slab"), lax.axis_size("dp")
    _, channels, height, cols = lattice_field.shape
    _, own_fine, half, _, _ = fine_kernels.shape
    _, own_coarse, mc, _, _ = coarse_kernels.shape
    cc, width = 2 * mc, cols // 2
    patch, cpatch = 9 * half, 9 * mc
    padded = round_up(patch, LANES)
    site_count = height * slabs * cols
    window = min(slabs, 11)

    field = lattice_field.reshape(channels, height, cols // LANES, LANES)
    field = jnp.transpose(field, (0, 2, 1, 3)).reshape(-1, LANES)
    fine_in = jnp.transpose(fine_kernels, (0, 3, 4, 1, 2)).reshape(2, 9, own_fine, half)
    coarse_in = jnp.transpose(coarse_kernels, (0, 3, 4, 1, 2)).reshape(2, 9, own_coarse, mc)

    pad_fine = round_up(own_fine, 8)
    tall = channels * height * cols // LANES
    copies = 3 * (shards - 1) + 6 + (window - 1) + 2 * (slabs - 1)
    vmem = pl.BlockSpec(memory_space=pltpu.VMEM)
    shapes = (
        jax.ShapeDtypeStruct((tall, LANES), F32),
        jax.ShapeDtypeStruct((cc * width // LANES, LANES), F32),
        jax.ShapeDtypeStruct((1, 1), F32),
        jax.ShapeDtypeStruct((2, 9, own_fine, half), F32),
        jax.ShapeDtypeStruct((2, 9, own_coarse, mc), F32),
    )
    results = pl.pallas_call(
        functools.partial(
            flow_kernel, slabs, shards, window, own_fine, own_coarse, site_count
        ),
        out_shape=shapes,
        in_specs=[pl.BlockSpec(memory_space=pltpu.HBM)] * 3,
        out_specs=(vmem,) * 5,
        scratch_shapes=[
            pltpu.VMEM(field.shape, BF16),
            pltpu.VMEM(fine_in.shape, BF16),
            pltpu.VMEM(coarse_in.shape, BF16),
            pltpu.VMEM(field.shape, F32),
            pltpu.VMEM((2, channels, cols), F32),
            pltpu.VMEM((2, half, cols), BF16),
            pltpu.VMEM((shards, 2, pad_fine, padded), F32),
            pltpu.VMEM((2, half, padded), F32),
            pltpu.VMEM((2, mc, LANES), F32),
            pltpu.VMEM((2, half, cols), BF16),
            pltpu.VMEM((2, half, cols), BF16),
            pltpu.VMEM((2, half, cols), BF16),
            pltpu.VMEM((12 * half, cols), BF16),
            pltpu.VMEM((12 * half, cols), BF16),
            pltpu.VMEM((12 * half, cols), BF16),
            pltpu.VMEM((2, channels, cols), F32),
            pltpu.VMEM((2, half, cols), F32),
            pltpu.VMEM((2, half, cols), F32),
            pltpu.VMEM((window, cc, width), F32),
            pltpu.VMEM((2, half, cols), BF16),
            pltpu.VMEM((2, half + cc, cols), BF16),
            pltpu.VMEM((2, half + cc, cols), BF16),
            pltpu.VMEM((shards, pad_fine, padded), F32),
            pltpu.VMEM((shards, pad_fine, padded), F32),
            pltpu.VMEM((shards - 1, pad_fine, padded), F32),
            pltpu.VMEM((shards - 1, pad_fine, padded), F32),
            pltpu.VMEM((slabs, pad_fine, padded), F32),
            pltpu.VMEM((slabs, pad_fine, padded), F32),
            pltpu.SemaphoreType.DMA((3,)),
            pltpu.SemaphoreType.DMA((copies,)),
            pltpu.SemaphoreType.DMA((copies,)),
        ],
        compiler_params=pltpu.CompilerParams(
            collective_id=0, has_side_effects=True, vmem_limit_bytes=40 * 1024 * 1024
        ),
    )(field, fine_in, coarse_in)
    lat, coarse, dens, fine, coarse_grads = pl.pallas_call(
        store_kernel,
        out_shape=shapes,
        in_specs=[pl.BlockSpec(memory_space=pl.ANY)] * 5,
        out_specs=(pl.BlockSpec(memory_space=pltpu.HBM),) * 5,
        scratch_shapes=[pltpu.SemaphoreType.DMA((5,))],
        compiler_params=pltpu.CompilerParams(vmem_limit_bytes=1024 * 1024),
    )(*results)

    lat = jnp.transpose(lat.reshape(channels, cols // LANES, height, LANES), (0, 2, 1, 3))
    return (
        lat.reshape(1, channels, height, cols),
        coarse.reshape(1, cc, 1, width),
        dens.reshape(1),
        jnp.transpose(fine.reshape(2, 3, 3, own_fine, half), (0, 3, 4, 1, 2)),
        jnp.transpose(coarse_grads.reshape(2, 3, 3, own_coarse, mc), (0, 3, 4, 1, 2)),
    )


def solution(mesh):
    from jax.sharding import PartitionSpec as P

    in_specs = (
        P(("groups", "dp"), None, "slab", None),
        P(None, "dp", None, None, None),
        P(None, "dp", None, None, None),
    )
    out_specs = (
        P(("groups", "dp"), None, "slab", None),
        P(("groups", "dp"), None, "slab", None),
        P(("groups", "dp")),
        P("groups", "dp", None, None, None),
        P("groups", "dp", None, None, None),
    )
    return jax.shard_map(
        on_device, mesh=mesh, in_specs=in_specs, out_specs=out_specs, check_vma=False
    )
```
